128 devices in a mesh: gx: 16 (over x_hi, y, core), gy: 8 (over z, x_lo).
Axes of the slice: x: 4 (x_hi: 2, x_lo: 2; x = x_hi * 2 + x_lo), y: 4, z: 4, core: 2. Of those that a mesh axis runs over, the one named last changes fastest.
Arguments:
- incident: bfloat16 [6, 256, 128, 192], P(None, 'gx', 'gy'), may hold values from -6 to 6
- adjoint_source: bfloat16 [6, 256, 128, 192], P(None, 'gx', 'gy'), may hold values from -6 to 6
- cell_class: int32 [256, 128], P('gx', 'gy'), may hold values from 0 to 7
- slot_table: int32 [8, 8], replicated, may hold values from 0 to 7, each once within a row
- gain_table: float32 [8, 8, 192], replicated, may hold values from 0.3 to 1.5
- admittance: float32 [8, 192], replicated, may hold values from 0.5 to 1.5
- coupling: bfloat16 [8, 192, 192], replicated, may hold values from -0.109375 to 0.109375
- self_inverse: bfloat16 [192, 192], replicated, may hold values from -0.15 to 1.21
Outputs:
- current: bfloat16 [6, 256, 128, 192], P(None, 'gx', 'gy')
- adjoint_state: bfloat16 [6, 256, 128, 192], P(None, 'gx', 'gy')
The draws below stay inside these ranges and needn't reach their ends.
All inputs are finite; a program needn't handle non-finite values.
Results may differ from the reference program's by a relative error of at most 0.02.
Values may be sent and summed in bfloat16 or wider, within the bound.
A program may use at most 128 MiB of HBM per device.

```python
import math
import jax
import jax.numpy as jnp
from jax import lax

U = 192
DIRS = 8
CLASSES = 8
SWEEPS = 3
R = 6
NX = 256
NY = 128


def draw_self_inverse(key, part):
    key = jax.random.fold_in(key, 7)
    first_key, second_key = jax.random.split(key)
    diagonal = jax.random.uniform(first_key, (U,), jnp.float32, 0.8, 1.2)
    spread = jnp.clip(jax.random.normal(second_key, (U, U), jnp.float32) * (0.5 / U ** 0.5), -0.148, 0.148)
    identity = jnp.eye(U, dtype=jnp.float32)
    return (spread * (1.0 - identity) + identity * diagonal[None, :]).astype(jnp.bfloat16)


def set_ends(values, rng, smallest, largest):
    longest = values.shape.index(max(values.shape))
    spots = []
    for shift in (0, 1):
        where = [jax.random.randint(jax.random.fold_in(rng, axis), (), 0, length) for axis, length in enumerate(values.shape)]
        where[longest] = (where[longest] + shift) % values.shape[longest]
        spots.append(tuple(where))
    return values.at[spots[0]].set(smallest).at[spots[1]].set(largest)


def levels(rng, extent, cuts, least, high):
    def one(position, blocks):
        heights = jax.random.uniform(jax.random.fold_in(jax.random.fold_in(rng, 6), position), (blocks,), jnp.float32, least / len(cuts), high / len(cuts))
        return jnp.repeat(jnp.exp(heights), extent[position] // blocks).reshape((-1,) + (1,) * (len(extent) - position - 1))

    loudness = one(*cuts[0])
    for cut in cuts[1:]:
        loudness = loudness * one(*cut)
    return loudness


def normal_values(own_key, shape, deviation, bound, pieces=(), kind=jnp.bfloat16):
    level = levels(own_key, shape, pieces, -0.22, 0.18) if pieces else 1.0
    array = jax.random.normal(own_key, shape, jnp.float32) * deviation * level
    return jnp.minimum(jnp.maximum(array, -bound), bound).astype(kind)


def setup_inputs(seed: int = 0) -> dict:
    streams_of = jax.random.split(jax.random.key(seed), 9)
    incident = normal_values(streams_of[0], (R, NX, NY, U), 1.0, 6.0, ((1, 16), (2, 8)))
    adjoint_source = normal_values(streams_of[1], (R, NX, NY, U), 1.0, 6.0, ((1, 16), (2, 8)))
    cell_class = set_ends(jax.random.randint(streams_of[2], (NX, NY), 0, CLASSES), jax.random.fold_in(streams_of[2], 1), 0, CLASSES - 1).astype(jnp.int32)
    slot_table = jax.vmap(lambda own: jax.random.permutation(own, DIRS))(jax.random.split(streams_of[3], CLASSES)).reshape((CLASSES, DIRS)).astype(jnp.int32)
    gain_table = jnp.clip(jnp.exp(jax.random.uniform(streams_of[4], (CLASSES, DIRS, U), jnp.float32, math.log(0.3), math.log(1.5))), 0.3, 1.5)
    admittance = jnp.clip(jnp.exp(jax.random.uniform(streams_of[5], (CLASSES, U), jnp.float32, math.log(0.5), math.log(1.5))), 0.5, 1.5)
    coupling = normal_values(streams_of[6], (DIRS, U, U), (16 * U) ** -0.5, 0.109375)
    self_inverse = draw_self_inverse(jax.random.fold_in(streams_of[8], 71), 0)
    return dict(incident=incident, adjoint_source=adjoint_source, cell_class=cell_class, slot_table=slot_table, gain_table=gain_table, admittance=admittance, coupling=coupling, self_inverse=self_inverse)


stencil_steps = ((-1, -1), (-1, 0), (-1, 1), (0, -1), (0, 1), (1, -1), (1, 0), (1, 1))


def product(operand, matrix):
    flat = operand.reshape(-1, operand.shape[-1])
    result = jnp.dot(flat, matrix, preferred_element_type=jnp.float32)
    return result.reshape(operand.shape[:-1] + (matrix.shape[1],))


def reference(incident, adjoint_source, cell_class, slot_table, gain_table, admittance, coupling, self_inverse):
    effective = gain_table[jnp.arange(CLASSES)[:, None], slot_table]
    cell_gains = [effective[:, direction][cell_class] for direction in range(DIRS)]
    admit_cell = admittance[cell_class]
    inverse_back = self_inverse.T

    def solve_one(fields):
        incident_one, source_one = fields
        current = (product(incident_one, self_inverse) * admit_cell).astype(jnp.bfloat16)
        adjoint_state = product((source_one * admit_cell).astype(jnp.bfloat16), inverse_back).astype(jnp.bfloat16)
        for sweep_step in range(SWEEPS):
            padded = jnp.pad(current, ((1, 1), (1, 1), (0, 0)))
            summed = jnp.zeros((NX, NY, U), jnp.float32)
            for direction, (shift_x, shift_y) in enumerate(stencil_steps):
                nearby = padded[1 + shift_x:1 + shift_x + NX, 1 + shift_y:1 + shift_y + NY]
                scaled = (nearby * cell_gains[direction]).astype(jnp.bfloat16)
                summed = summed + product(scaled, coupling[direction])
            remainder = (incident_one.astype(jnp.float32) - summed).astype(jnp.bfloat16)
            far_sum = jnp.zeros((NX, NY, U), jnp.float32)
            for direction, (shift_x, shift_y) in enumerate(stencil_steps):
                partial_value = (product(adjoint_state, coupling[direction].T) * cell_gains[direction]).astype(jnp.bfloat16)
                moved = jnp.pad(partial_value.astype(jnp.float32), ((1, 1), (1, 1), (0, 0)))
                far_sum = far_sum + moved[1 - shift_x:1 - shift_x + NX, 1 - shift_y:1 - shift_y + NY]
            back = ((source_one.astype(jnp.float32) - far_sum) * admit_cell).astype(jnp.bfloat16)
            current = (product(remainder, self_inverse) * admit_cell).astype(jnp.bfloat16)
            adjoint_state = product(back, inverse_back).astype(jnp.bfloat16)
        return current, adjoint_state

    current, adjoint_state = lax.map(solve_one, (incident, adjoint_source))
    return current, adjoint_state
```

```python
import functools

import jax
import jax.numpy as jnp
from jax import lax
from jax.experimental import pallas as pl
from jax.experimental.pallas import tpu as pltpu
from jax.sharding import PartitionSpec as P

MESH = pl.DeviceIdType.MESH
F32 = jnp.float32
BF16 = jnp.bfloat16
SWEEPS = 3
R = 6
N = 16
ROWS = N * N
EDGE = R * N
U = 192
T = 128
HALF = 64
STEPS = ((-1, -1), (-1, 0), (-1, 1), (0, -1), (0, 1), (1, -1), (1, 0), (1, 1))
PAIRS = ((0, 5), (1, 6), (2, 7), (3, 4))
TILES = 12
Y_DIRS = ((0, 3, 5), (2, 4, 7))
X_DIRS = ((0, 1, 2), (5, 6, 7))
Y_TILES = ((0, 3, 5, 8, 11), (2, 4, 7, 10, 11))
X_TILES = ((0, 1, 2, 8, 9, 10), (5, 6, 7, 8, 9, 10))


def dot(a, b):
    return jnp.dot(a, b, preferred_element_type=F32)


def dot_nt(a, b):
    return lax.dot_general(a, b, (((1,), (1,)), ((), ())), preferred_element_type=F32)


def iota(shape, dim):
    return lax.broadcasted_iota(jnp.int32, shape, dim)


def low(rows):
    return iota((rows, T), 1) < HALF


def turn(x, shift, axis=0):
    size = x.shape[axis]
    return x if shift % size == 0 else pltpu.roll(x, shift % size, axis)


def spread(tile, corner=None):
    return jnp.concatenate([tile] * R + ([] if corner is None else [corner]), axis=0)


def fold(tile):
    return tile + turn(tile, HALF, 1)


def kernel(
    nx, ny,
    inc, src, cls, slot, gain, adm, coup, sinv,
    cur_out, adj_out,
    v0, vm, vp, adj, near_a, near_h, far_a, far_h, gains, lhs, weights, weights_t, partial,
    admit, admit_e, inc_e, src_e, gains_y, gains_x, solve, solve_t, solve_tn, corner_s,
    send_y, send_x, send_c, recv_y, recv_x, recv_c,
    send_sem, recv_sem,
):
    gx, gy = lax.axis_index("gx"), lax.axis_index("gy")
    left, right = lax.rem(gx + nx - 1, nx), lax.rem(gx + 1, nx)
    down, up = lax.rem(gy + ny - 1, ny), lax.rem(gy + 1, ny)
    y_to = ((gx, down), (gx, up))
    x_to = ((left, gy), (right, gy))
    c_to = ((left, down), (right, down), (left, up), (right, up))

    barrier = pltpu.get_barrier_semaphore()
    for where in y_to + x_to + c_to:
        pl.semaphore_signal(barrier, inc=1, device_id=where, device_id_type=MESH)

    one = jnp.float32(1.0)
    has_left, has_right = jnp.where(gx > 0, 1.0, 0.0) * one, jnp.where(gx < nx - 1, 1.0, 0.0) * one
    has_down, has_up = jnp.where(gy > 0, 1.0, 0.0) * one, jnp.where(gy < ny - 1, 1.0, 0.0) * one

    def chooser(rows, columns, wanted):
        return jnp.where(iota((rows, columns), 0) == wanted, 1.0, 0.0).astype(BF16)

    lane = iota((U, 2 * T), 1)
    dup = chooser(U, 2 * T, jnp.where(lane < U, lane, lane - HALF))
    dup_back = chooser(U, 2 * T, jnp.where(lane < HALF, lane + T, jnp.where(lane < T, lane + HALF, lane - T)))
    eye = chooser(U, U, iota((U, U), 1))
    solve[...] = dot(sinv[...], dup).astype(BF16)
    solve_n = dot_nt(eye, sinv[...]).astype(BF16)
    solve_tn[...] = solve_n
    solve_t[...] = dot(solve_n, dup_back).astype(BF16)

    weights[...] = jnp.zeros_like(weights)
    for d in range(8):
        weights[d * T:(d + 1) * T, 0:U] = coup[d, 0:T, :]
    for p, (d0, d1) in enumerate(PAIRS):
        base = (8 + p) * T
        weights[base:base + HALF, 0:U] = coup[d0, T:U, :]
        weights[base + HALF:base + T, 0:U] = coup[d1, T:U, :]
    row = iota((2 * T, U), 0)
    place = jnp.where(row < HALF, -1, jnp.where(row < T, row + HALF, row - T))
    order = jnp.where(iota((2 * T, U), 1) == place, 1.0, 0.0).astype(BF16)
    for t in range(TILES):
        weights_t[:, t * T:(t + 1) * T] = dot_nt(order, weights[t * T:(t + 1) * T, 0:U]).astype(BF16)

    pick = [
        jnp.where(iota((8, 64), 1) == iota((8, 64), 0) * 8 + slot[:, d:d + 1], 1.0, 0.0)
        for d in range(8)
    ]
    pick = jnp.concatenate(pick, axis=0).astype(BF16)
    gain_dup = dot(gain[...].astype(BF16), dup).astype(BF16)
    table64 = dot(pick, gain_dup)
    pieces = [table64[d * 8:(d + 1) * 8, 0:T] for d in range(8)]
    for d0, d1 in PAIRS:
        pieces.append(jnp.where(low(8), table64[d0 * 8:(d0 + 1) * 8, T:], table64[d1 * 8:(d1 + 1) * 8, T:]))
    table = jnp.concatenate(pieces, axis=1)
    table = jnp.concatenate([table, jnp.zeros_like(table)], axis=0).astype(BF16)
    adm_high = adm[...].astype(BF16).astype(F32)
    adm_both = jnp.concatenate([adm_high, adm[...] - adm_high], axis=0).astype(BF16)
    adm_table = dot(adm_both, dup).astype(BF16)

    diag = iota((N, N), 0) == iota((N, N), 1)
    spots = [jnp.where(diag, cls[x:x + 1, :].astype(F32), 0.0) for x in range(N)]
    kind = dot(jnp.concatenate(spots, axis=0).astype(BF16), jnp.ones((N, N), BF16))

    def onehot(kinds):
        which = lax.rem(iota((kinds.shape[0], N), 1), 8)
        return jnp.where(which.astype(F32) == kinds, 1.0, 0.0).astype(BF16)

    kind_e = jnp.concatenate(
        [
            jnp.broadcast_to(cls[:, 0:1].astype(F32), (N, N)),
            jnp.broadcast_to(cls[:, N - 1:N].astype(F32), (N, N)),
            kind[0:N],
            kind[ROWS - N:ROWS],
        ],
        axis=0,
    )
    hot, hot_e = onehot(kind), onehot(kind_e)
    admit[...] = dot(hot, adm_table)
    admit_e[...] = dot(hot_e, adm_table)

    def inside(rows, sx, sy):
        r = iota((rows, T), 0)
        x, y = r // N + sx, lax.rem(r, N) + sy
        return (x >= 0) & (x < N) & (y >= 0) & (y < N)

    for t in range(TILES):
        value = dot(hot, table[:, t * T:(t + 1) * T])
        if t < 8:
            keep = jnp.where(inside(ROWS, *STEPS[t]), 1.0, 0.0)
        else:
            d0, d1 = PAIRS[t - 8]
            keep = jnp.where(
                low(ROWS), jnp.where(inside(ROWS, *STEPS[d0]), 1.0, 0.0), jnp.where(inside(ROWS, *STEPS[d1]), 1.0, 0.0)
            )
        gains[:, t * T:(t + 1) * T] = (value * keep).astype(BF16)

    edge_gain = dot(hot_e, table)
    spot = iota((N, T), 0)

    def along(j):
        return jnp.where((spot + j >= 0) & (spot + j < N), 1.0, 0.0)

    lows = jnp.where(low(N), 1.0, 0.0)
    for e, exists in enumerate((has_down, has_up)):
        raw = edge_gain[e * N:(e + 1) * N]
        first = jnp.where(spot < 8, 1.0, 0.0)
        side = first * has_left + (1.0 - first) * has_right
        for k, t in enumerate(Y_TILES[e]):
            tile = raw[:, t * T:(t + 1) * T]
            ends = jnp.where(spot < 8, jnp.broadcast_to(tile[0:1], (N, T)), jnp.broadcast_to(tile[N - 1:N], (N, T)))
            if k < 3:
                keep = along(k - 1)
                corner = (first, 0.0 * first, 1.0 - first)[k]
            elif k == 3:
                keep = lows * along(-1) + (1.0 - lows) * along(1)
                corner = lows * first + (1.0 - lows) * (1.0 - first)
            else:
                keep = lows if e == 0 else 1.0 - lows
                corner = 0.0 * first
            gains_y[e, 0:N, k * T:(k + 1) * T] = tile * keep * exists
            gains_y[e, N:2 * N, k * T:(k + 1) * T] = ends * corner * side * exists
    for e, exists in enumerate((has_left, has_right)):
        raw = edge_gain[(2 + e) * N:(3 + e) * N]
        for k, t in enumerate(X_TILES[e]):
            keep = along(k % 3 - 1)
            if k >= 3:
                keep = keep * (lows if e == 0 else 1.0 - lows)
            gains_x[e, :, k * T:(k + 1) * T] = raw[:, t * T:(t + 1) * T] * keep * exists

    for data, a_ref, h_ref, e_ref in ((inc, near_a, near_h, inc_e), (src, far_a, far_h, src_e)):
        h_ref[...] = jnp.zeros_like(h_ref)
        for r in range(R):
            a_ref[r * ROWS:(r + 1) * ROWS, :] = data[r, :, 0:T].astype(F32)
            h_ref[r * ROWS:(r + 1) * ROWS, 0:HALF] = data[r, :, T:U].astype(F32)
        for k, ref in enumerate((a_ref, h_ref)):
            columns = slice(k * T, (k + 1) * T)
            for e in range(2):
                e_ref[e * EDGE:(e + 1) * EDGE, columns] = ref[pl.ds(e * (N - 1), EDGE, stride=N), :]
                for r in range(R):
                    at = (2 + e) * EDGE + r * N
                    start = r * ROWS + e * (ROWS - N)
                    e_ref[at:at + N, columns] = ref[start:start + N, :]
            ref[...] = jnp.zeros_like(ref)
    for ref in (v0, vm, vp):
        for r in range(R):
            ref[r, 0:N, :] = jnp.zeros((N, 2 * T), BF16)
            ref[r, (N + 1) * N:(N + 2) * N, :] = jnp.zeros((N, 2 * T), BF16)
    partial[0:N, :] = jnp.zeros((N, TILES * T), BF16)
    partial[(N + 1) * N:(N + 2) * N, :] = jnp.zeros((N, TILES * T), BF16)
    corner_s[...] = jnp.zeros_like(corner_s)

    def take(ref):
        parts = [ref[pl.ds(e * (N - 1), EDGE, stride=N), :] for e in range(2)]
        for e in range(2):
            for r in range(R):
                start = r * ROWS + e * (ROWS - N)
                parts.append(ref[start:start + N, :])
        return jnp.concatenate(parts, axis=0)

    def solve_edges(v):
        scale = jnp.concatenate([spread(admit_e[e * N:(e + 1) * N, :]) for e in range(4)], axis=0)
        near_e = jnp.concatenate([take(near_a), take(near_h)], axis=1)
        rest = (inc_e[...] - near_e).astype(BF16)
        cur_e = dot(rest[:, 0:U], solve[...]) * scale
        far_e = jnp.concatenate([take(far_a), take(far_h)], axis=1)
        back = ((src_e[...] - far_e) * scale).astype(BF16)
        adj_e = dot(back[:, 0:U], solve_t[...])

        for e in range(2):
            rows = slice(e * EDGE, (e + 1) * EDGE)
            corner_s[0, 0:EDGE, :] = cur_e[rows, 0:T]
            corner_s[1, 0:EDGE, :] = cur_e[rows, T:]
            corner_s[2, 0:EDGE, :] = adj_e[rows, 0:T]
            corner_s[3, 0:EDGE, :] = adj_e[rows, T:]
            cut = [
                jnp.concatenate([corner_s[k, pl.ds(0, 8, stride=N), :], corner_s[k, pl.ds(N - 1, 8, stride=N), :]], axis=0)
                for k in range(4)
            ]
            state = jnp.concatenate([adj_e[rows], jnp.concatenate(cut[2:], axis=1)], axis=0).astype(BF16)
            out = []
            for k, t in enumerate(Y_TILES[e]):
                gain_k = gains_y[e, :, k * T:(k + 1) * T]
                out.append(dot(state, weights_t[:, t * T:(t + 1) * T]) * spread(gain_k[0:N], gain_k[N:]))
            part_a = turn(out[0][:EDGE], -1) + out[1][:EDGE] + turn(out[2][:EDGE], 1)
            part_h = fold(
                jnp.where(low(EDGE), turn(out[3][:EDGE], -1), turn(out[3][:EDGE], 1)) + out[4][:EDGE]
            )
            tail_a = out[0][EDGE:] + out[1][EDGE:] + out[2][EDGE:]
            tail_h = fold(out[3][EDGE:] + out[4][EDGE:])
            message = jnp.concatenate(
                [cur_e[rows, 0:T], jnp.where(low(EDGE), cur_e[rows, T:], part_h), part_a], axis=1
            ).astype(BF16)
            send_y[v, e] = message.reshape(R, N, 3 * T)
            tail = jnp.concatenate([cut[0], jnp.where(low(N), cut[1], tail_h), tail_a], axis=1)
            send_c[v, 2 * e] = tail[0:8]
            send_c[v, 2 * e + 1] = tail[8:16]
        for e in range(2):
            rows = slice((2 + e) * EDGE, (3 + e) * EDGE)
            state = adj_e[rows].astype(BF16)
            out = []
            for k, t in enumerate(X_TILES[e]):
                out.append(dot(state, weights_t[:, t * T:(t + 1) * T]) * spread(gains_x[e, :, k * T:(k + 1) * T]))
            part_a = turn(out[0], -1) + out[1] + turn(out[2], 1)
            part_h = fold(turn(out[3], -1) + out[4] + turn(out[5], 1))
            message = jnp.concatenate(
                [cur_e[rows, 0:T], jnp.where(low(EDGE), cur_e[rows, T:], part_h), part_a], axis=1
            ).astype(BF16)
            send_x[v, e] = message.reshape(R, N, 3 * T)

    def copies(v):
        made = []
        for e in range(2):
            made.append((send_y.at[v, e], recv_y.at[v, 1 - e], y_to[e], e, 1 - e))
        for e in range(2):
            made.append((send_x.at[v, e], recv_x.at[v, 1 - e], x_to[e], 2 + e, 3 - e))
        for q in range(4):
            made.append((send_c.at[v, q], recv_c.at[v, 3 - q], c_to[q], 4 + q, 7 - q))
        return [
            pltpu.make_async_remote_copy(
                src_ref=a, dst_ref=b, send_sem=send_sem.at[v, s], recv_sem=recv_sem.at[v, t],
                device_id=where, device_id_type=MESH,
            )
            for a, b, where, s, t in made
        ]

    def right_sides(r):
        at = pl.ds(pl.multiple_of(r * ROWS, ROWS), ROWS)
        near = jnp.concatenate([near_a[at, :], near_h[at, 0:HALF]], axis=1)
        far = jnp.concatenate([far_a[at, :], far_h[at, 0:HALF]], axis=1)
        rest = (inc[r].astype(F32) - near).astype(BF16)
        back = ((src[r].astype(F32) - far) * admit[:, 0:U]).astype(BF16)
        return rest, back

    def solve_block(r, carry):
        rest, back = right_sides(r)
        cur = dot(rest, solve[...]) * admit[...]
        v0[r, N:N + ROWS, :] = cur.astype(BF16)
        vm[r, N:N + ROWS, :] = turn(cur, 1).astype(BF16)
        vp[r, N:N + ROWS, :] = turn(cur, -1).astype(BF16)
        adj[r] = dot(back, solve_t[...]).astype(BF16)
        return carry

    shifted = {-1: vm, 0: v0, 1: vp}

    def near_block(r, carry):
        def nearby(d, columns):
            sx, sy = STEPS[d]
            return shifted[sy][r, N * (1 + sx):N * (1 + sx) + ROWS, columns]

        for d in range(8):
            columns = slice(d * T, (d + 1) * T)
            lhs[:, columns] = nearby(d, slice(0, T)) * gains[:, columns]
        for p, (d0, d1) in enumerate(PAIRS):
            columns = slice((8 + p) * T, (9 + p) * T)
            both = jnp.where(low(ROWS), nearby(d0, slice(T, 2 * T)), nearby(d1, slice(T, 2 * T)))
            lhs[:, columns] = both * gains[:, columns]
        near = dot(lhs[...], weights[...])
        at = pl.ds(pl.multiple_of(r * ROWS, ROWS), ROWS)
        near_a[at, :] = near[:, 0:T]
        near_h[at, :] = near[:, T:]
        return carry

    def far_block(r, carry):
        for t in range(TILES // 2):
            columns = slice(2 * t * T, 2 * (t + 1) * T)
            value = dot(adj[r], weights_t[:, columns]).astype(BF16)
            partial[N:N + ROWS, columns] = value * gains[:, columns]

        def part(x, t):
            return partial[x * N:(x + 1) * N, t * T:(t + 1) * T].astype(F32)

        for x in range(N):
            sums = {sy: None for sy in (-1, 0, 1)}
            for d, (sx, sy) in enumerate(STEPS):
                value = part(1 + x - sx, d)
                sums[sy] = value if sums[sy] is None else sums[sy] + value
            a = turn(sums[1], 1) + sums[0] + turn(sums[-1], -1)
            tops = {sy: jnp.where(low(N), part(2 + x, 9 + sy), part(x, 9 + sy)) for sy in (-1, 0, 1)}
            mid = part(1 + x, 11)
            below = tops[-1] + jnp.where(low(N), mid, 0.0)
            above = tops[1] + jnp.where(low(N), 0.0, mid)
            h = fold(turn(above, 1) + tops[0] + turn(below, -1))
            at = pl.ds(pl.multiple_of(r * ROWS + x * N, N), N)
            far_a[at, :] = a
            far_h[at, :] = h
        return carry

    def correct(v):
        for e in range(2):
            whole = jnp.concatenate(
                [recv_y[v, e].reshape(EDGE, 3 * T).astype(F32), recv_c[v, 2 * e], recv_c[v, 2 * e + 1]], axis=0
            )
            rows = EDGE + N
            a, mixed, part_a = whole[:, 0:T], whole[:, T:2 * T], whole[:, 2 * T:]
            other = turn(mixed, HALF, 1)
            h = jnp.where(low(rows), mixed, other)

            def moved(x, j):
                return jnp.concatenate([turn(x[:EDGE], -j), x[EDGE:]], axis=0)

            tiles = [moved(a, -1), a, moved(a, 1), jnp.where(low(rows), moved(h, -1), moved(h, 1)), h]
            scaled = []
            for k, tile in enumerate(tiles):
                gain_k = gains_y[e, :, k * T:(k + 1) * T]
                scaled.append((tile * spread(gain_k[0:N], gain_k[N:])).astype(BF16))
            matrix = jnp.concatenate([weights[t * T:(t + 1) * T, :] for t in Y_TILES[e]], axis=0)
            extra = dot(jnp.concatenate(scaled, axis=1), matrix)
            for ref, value in (
                (near_a, extra[:, 0:T]), (near_h, extra[:, T:]), (far_a, part_a), (far_h, other)
            ):
                y0 = e * (N - 1)
                for at, piece in (
                    (pl.ds(y0, EDGE, stride=N), value[:EDGE]),
                    (pl.ds(y0, 8, stride=ROWS), value[EDGE:EDGE + 8]),
                    (pl.ds(y0 + ROWS - N, 8, stride=ROWS), value[EDGE + 8:]),
                ):
                    ref[at, :] = ref[at, :] + piece
        for e in range(2):
            whole = recv_x[v, e].reshape(EDGE, 3 * T).astype(F32)
            a, mixed, part_a = whole[:, 0:T], whole[:, T:2 * T], whole[:, 2 * T:]
            other = turn(mixed, HALF, 1)
            h = mixed if e == 0 else other
            tiles = [turn(a, 1), a, turn(a, -1), turn(h, 1), h, turn(h, -1)]
            scaled = []
            for k, tile in enumerate(tiles):
                scaled.append((tile * spread(gains_x[e, :, k * T:(k + 1) * T])).astype(BF16))
            matrix = jnp.concatenate([weights[t * T:(t + 1) * T, :] for t in X_TILES[e]], axis=0)
            extra = dot(jnp.concatenate(scaled, axis=1), matrix)
            for ref, value in (
                (near_a, extra[:, 0:T]), (near_h, extra[:, T:]), (far_a, part_a), (far_h, other)
            ):
                for r in range(R):
                    start = r * ROWS + e * (ROWS - N)
                    ref[start:start + N, :] = ref[start:start + N, :] + value[r * N:(r + 1) * N]

    pl.semaphore_wait(barrier, 8)

    def sweep(v, carry):
        solve_edges(v)
        for copy in copies(v):
            copy.start()
        lax.fori_loop(0, R, solve_block, 0)
        lax.fori_loop(0, R, near_block, 0)
        lax.fori_loop(0, R, far_block, 0)
        for copy in copies(v):
            copy.wait_recv()
        correct(v)
        for copy in copies(v):
            copy.wait_send()
        return carry

    lax.fori_loop(0, SWEEPS, sweep, 0)

    def finish(r, carry):
        rest, back = right_sides(r)
        cur = dot(rest, solve[...]) * admit[...]
        cur_out[r] = cur[:, 0:U].astype(BF16)
        adj_out[r] = dot(back, solve_tn[...]).astype(BF16)
        return carry

    lax.fori_loop(0, R, finish, 0)


def solution(mesh):
    nx, ny = mesh.shape["gx"], mesh.shape["gy"]

    def local(inc, src, cls, slot, gain, adm, coup, sinv):
        vmem = pl.BlockSpec(memory_space=pltpu.VMEM)
        out = jax.ShapeDtypeStruct((R, ROWS, U), BF16)
        cur, adj = pl.pallas_call(
            functools.partial(kernel, nx, ny),
            out_shape=(out, out),
            in_specs=[vmem] * 8,
            out_specs=(vmem, vmem),
            scratch_shapes=[
                pltpu.VMEM((R, ROWS + 2 * N, 2 * T), BF16),
                pltpu.VMEM((R, ROWS + 2 * N, 2 * T), BF16),
                pltpu.VMEM((R, ROWS + 2 * N, 2 * T), BF16),
                pltpu.VMEM((R, ROWS, 2 * T), BF16),
                pltpu.VMEM((8 * ROWS, T), F32),
                pltpu.VMEM((8 * ROWS, T), F32),
                pltpu.VMEM((8 * ROWS, T), F32),
                pltpu.VMEM((8 * ROWS, T), F32),
                pltpu.VMEM((ROWS, TILES * T), BF16),
                pltpu.VMEM((ROWS, TILES * T), BF16),
                pltpu.VMEM((TILES * T, 2 * T), BF16),
                pltpu.VMEM((2 * T, TILES * T), BF16),
                pltpu.VMEM((ROWS + 2 * N, TILES * T), BF16),
                pltpu.VMEM((ROWS, 2 * T), F32),
                pltpu.VMEM((4 * N, 2 * T), F32),
                pltpu.VMEM((4 * EDGE, 2 * T), F32),
                pltpu.VMEM((4 * EDGE, 2 * T), F32),
                pltpu.VMEM((2, 2 * N, 5 * T), F32),
                pltpu.VMEM((2, N, 6 * T), F32),
                pltpu.VMEM((U, 2 * T), BF16),
                pltpu.VMEM((U, 2 * T), BF16),
                pltpu.VMEM((U, U), BF16),
                pltpu.VMEM((4, 8 * N, T), F32),
                pltpu.VMEM((SWEEPS, 2, R, N, 3 * T), BF16),
                pltpu.VMEM((SWEEPS, 2, R, N, 3 * T), BF16),
                pltpu.VMEM((SWEEPS, 4, 8, 3 * T), F32),
                pltpu.VMEM((SWEEPS, 2, R, N, 3 * T), BF16),
                pltpu.VMEM((SWEEPS, 2, R, N, 3 * T), BF16),
                pltpu.VMEM((SWEEPS, 4, 8, 3 * T), F32),
                pltpu.SemaphoreType.DMA((SWEEPS, 8)),
                pltpu.SemaphoreType.DMA((SWEEPS, 8)),
            ],
            compiler_params=pltpu.CompilerParams(
                collective_id=0, has_side_effects=True, vmem_limit_bytes=60 * 1024 * 1024
            ),
        )(
            inc.reshape(R, ROWS, U), src.reshape(R, ROWS, U), cls, slot, gain.reshape(64, U), adm, coup, sinv
        )
        return cur.reshape(R, N, N, U), adj.reshape(R, N, N, U)

    placed = (P(None, "gx", "gy", None), P(None, "gx", "gy", None), P("gx", "gy"), P(), P(), P(), P(), P())
    return jax.shard_map(
        local, mesh=mesh, in_specs=placed, out_specs=(placed[0], placed[0]), check_vma=False
    )
```

```python
import functools

import jax
import jax.numpy as jnp
from jax import lax
from jax.experimental import pallas as pl
from jax.experimental.pallas import tpu as pltpu
from jax.sharding import PartitionSpec as P

MESH = pl.DeviceIdType.MESH
F32 = jnp.float32
BF16 = jnp.bfloat16
SWEEPS = 3
R = 6
N = 16
ROWS = N * N
EDGE = R * N
U = 192
PER = 6
MANY = PER * ROWS
T = 128
HALF = 64
STEPS = ((-1, -1), (-1, 0), (-1, 1), (0, -1), (0, 1), (1, -1), (1, 0), (1, 1))
PAIRS = ((0, 5), (1, 6), (2, 7), (3, 4))
TILES = 12
Y_DIRS = ((0, 3, 5), (2, 4, 7))
X_DIRS = ((0, 1, 2), (5, 6, 7))
Y_TILES = ((0, 3, 5, 8, 11), (2, 4, 7, 10, 11))
X_TILES = ((0, 1, 2, 8, 9, 10), (5, 6, 7, 8, 9, 10))


def dot(a, b):
    return jnp.dot(a, b, preferred_element_type=F32)


def dot_nt(a, b):
    return lax.dot_general(a, b, (((1,), (1,)), ((), ())), preferred_element_type=F32)


def iota(shape, dim):
    return lax.broadcasted_iota(jnp.int32, shape, dim)


def low(rows):
    return iota((rows, T), 1) < HALF


def turn(x, shift, axis=0):
    size = x.shape[axis]
    return x if shift % size == 0 else pltpu.roll(x, shift % size, axis)


def spread(tile, corner=None):
    return jnp.concatenate([tile] * R + ([] if corner is None else [corner]), axis=0)


def fold(tile):
    return tile + turn(tile, HALF, 1)


def kernel(
    nx, ny,
    inc, src, cls, slot, gain, adm, coup, sinv,
    cur_out, adj_out,
    v0, vm, vp, adj, near_a, near_h, far_a, far_h, gains, lhs, weights, weights_t, partial,
    admit, admit_e, inc_e, src_e, gains_y, gains_x, solve, solve_t, solve_tn, corner_s,
    send_y, send_x, send_c, recv_y, recv_x, recv_c,
    send_sem, recv_sem,
):
    gx, gy = lax.axis_index("gx"), lax.axis_index("gy")
    left, right = lax.rem(gx + nx - 1, nx), lax.rem(gx + 1, nx)
    down, up = lax.rem(gy + ny - 1, ny), lax.rem(gy + 1, ny)
    y_to = ((gx, down), (gx, up))
    x_to = ((left, gy), (right, gy))
    c_to = ((left, down), (right, down), (left, up), (right, up))

    barrier = pltpu.get_barrier_semaphore()
    for where in y_to + x_to + c_to:
        pl.semaphore_signal(barrier, inc=1, device_id=where, device_id_type=MESH)

    one = jnp.float32(1.0)
    has_left, has_right = jnp.where(gx > 0, 1.0, 0.0) * one, jnp.where(gx < nx - 1, 1.0, 0.0) * one
    has_down, has_up = jnp.where(gy > 0, 1.0, 0.0) * one, jnp.where(gy < ny - 1, 1.0, 0.0) * one

    def chooser(rows, columns, wanted):
        return jnp.where(iota((rows, columns), 0) == wanted, 1.0, 0.0).astype(BF16)

    lane = iota((U, 2 * T), 1)
    dup = chooser(U, 2 * T, jnp.where(lane < U, lane, lane - HALF))
    dup_back = chooser(U, 2 * T, jnp.where(lane < HALF, lane + T, jnp.where(lane < T, lane + HALF, lane - T)))
    eye = chooser(U, U, iota((U, U), 1))
    solve[...] = dot(sinv[...], dup).astype(BF16)
    solve_n = dot_nt(eye, sinv[...]).astype(BF16)
    solve_tn[...] = solve_n
    solve_t[...] = dot(solve_n, dup_back).astype(BF16)

    weights[...] = jnp.zeros_like(weights)
    for d in range(8):
        weights[d * T:(d + 1) * T, 0:U] = coup[d, 0:T, :]
    for p, (d0, d1) in enumerate(PAIRS):
        base = (8 + p) * T
        weights[base:base + HALF, 0:U] = coup[d0, T:U, :]
        weights[base + HALF:base + T, 0:U] = coup[d1, T:U, :]
    row = iota((2 * T, U), 0)
    place = jnp.where(row < HALF, -1, jnp.where(row < T, row + HALF, row - T))
    order = jnp.where(iota((2 * T, U), 1) == place, 1.0, 0.0).astype(BF16)
    for t in range(TILES):
        weights_t[:, t * T:(t + 1) * T] = dot_nt(order, weights[t * T:(t + 1) * T, 0:U]).astype(BF16)

    pick = [
        jnp.where(iota((8, 64), 1) == iota((8, 64), 0) * 8 + slot[:, d:d + 1], 1.0, 0.0)
        for d in range(8)
    ]
    pick = jnp.concatenate(pick, axis=0).astype(BF16)
    gain_dup = dot(gain[...].astype(BF16), dup).astype(BF16)
    table64 = dot(pick, gain_dup)
    pieces = [table64[d * 8:(d + 1) * 8, 0:T] for d in range(8)]
    for d0, d1 in PAIRS:
        pieces.append(jnp.where(low(8), table64[d0 * 8:(d0 + 1) * 8, T:], table64[d1 * 8:(d1 + 1) * 8, T:]))
    table = jnp.concatenate(pieces, axis=1)
    table = jnp.concatenate([table, jnp.zeros_like(table)], axis=0).astype(BF16)
    adm_high = adm[...].astype(BF16).astype(F32)
    adm_both = jnp.concatenate([adm_high, adm[...] - adm_high], axis=0).astype(BF16)
    adm_table = dot(adm_both, dup).astype(BF16)

    diag = iota((N, N), 0) == iota((N, N), 1)
    spots = [jnp.where(diag, cls[x:x + 1, :].astype(F32), 0.0) for x in range(N)]
    kind = dot(jnp.concatenate(spots, axis=0).astype(BF16), jnp.ones((N, N), BF16))

    def onehot(kinds):
        which = lax.rem(iota((kinds.shape[0], N), 1), 8)
        return jnp.where(which.astype(F32) == kinds, 1.0, 0.0).astype(BF16)

    kind_e = jnp.concatenate(
        [
            jnp.broadcast_to(cls[:, 0:1].astype(F32), (N, N)),
            jnp.broadcast_to(cls[:, N - 1:N].astype(F32), (N, N)),
            kind[0:N],
            kind[ROWS - N:ROWS],
        ],
        axis=0,
    )
    hot, hot_e = onehot(kind), onehot(kind_e)
    admit[...] = dot(hot, adm_table)
    admit_e[...] = dot(hot_e, adm_table)

    def inside(rows, sx, sy):
        r = iota((rows, T), 0)
        x, y = r // N + sx, lax.rem(r, N) + sy
        return (x >= 0) & (x < N) & (y >= 0) & (y < N)

    for t in range(TILES):
        value = dot(hot, table[:, t * T:(t + 1) * T])
        if t < 8:
            keep = jnp.where(inside(ROWS, *STEPS[t]), 1.0, 0.0)
        else:
            d0, d1 = PAIRS[t - 8]
            keep = jnp.where(
                low(ROWS), jnp.where(inside(ROWS, *STEPS[d0]), 1.0, 0.0), jnp.where(inside(ROWS, *STEPS[d1]), 1.0, 0.0)
            )
        gains[:, t * T:(t + 1) * T] = (value * keep).astype(BF16)

    edge_gain = dot(hot_e, table)
    spot = iota((N, T), 0)

    def along(j):
        return jnp.where((spot + j >= 0) & (spot + j < N), 1.0, 0.0)

    lows = jnp.where(low(N), 1.0, 0.0)
    for e, exists in enumerate((has_down, has_up)):
        raw = edge_gain[e * N:(e + 1) * N]
        first = jnp.where(spot < 8, 1.0, 0.0)
        side = first * has_left + (1.0 - first) * has_right
        for k, t in enumerate(Y_TILES[e]):
            tile = raw[:, t * T:(t + 1) * T]
            ends = jnp.where(spot < 8, jnp.broadcast_to(tile[0:1], (N, T)), jnp.broadcast_to(tile[N - 1:N], (N, T)))
            if k < 3:
                keep = along(k - 1)
                corner = (first, 0.0 * first, 1.0 - first)[k]
            elif k == 3:
                keep = lows * along(-1) + (1.0 - lows) * along(1)
                corner = lows * first + (1.0 - lows) * (1.0 - first)
            else:
                keep = lows if e == 0 else 1.0 - lows
                corner = 0.0 * first
            gains_y[e, 0:N, k * T:(k + 1) * T] = tile * keep * exists
            gains_y[e, N:2 * N, k * T:(k + 1) * T] = ends * corner * side * exists
    for e, exists in enumerate((has_left, has_right)):
        raw = edge_gain[(2 + e) * N:(3 + e) * N]
        for k, t in enumerate(X_TILES[e]):
            keep = along(k % 3 - 1)
            if k >= 3:
                keep = keep * (lows if e == 0 else 1.0 - lows)
            gains_x[e, :, k * T:(k + 1) * T] = raw[:, t * T:(t + 1) * T] * keep * exists

    for data, a_ref, h_ref, e_ref in ((inc, near_a, near_h, inc_e), (src, far_a, far_h, src_e)):
        h_ref[...] = jnp.zeros_like(h_ref)
        for r in range(R):
            a_ref[r * ROWS:(r + 1) * ROWS, :] = data[r * ROWS:(r + 1) * ROWS, 0:T].astype(F32)
            h_ref[r * ROWS:(r + 1) * ROWS, 0:HALF] = data[r * ROWS:(r + 1) * ROWS, T:U].astype(F32)
        for k, ref in enumerate((a_ref, h_ref)):
            columns = slice(k * T, (k + 1) * T)
            for e in range(2):
                e_ref[e * EDGE:(e + 1) * EDGE, columns] = ref[pl.ds(e * (N - 1), EDGE, stride=N), :]
                for r in range(R):
                    at = (2 + e) * EDGE + r * N
                    start = r * ROWS + e * (ROWS - N)
                    e_ref[at:at + N, columns] = ref[start:start + N, :]
            ref[...] = jnp.zeros_like(ref)
    for ref in (v0, vm, vp):
        for r in range(R):
            ref[r, 0:N, :] = jnp.zeros((N, 2 * T), BF16)
            ref[r, (N + 1) * N:(N + 2) * N, :] = jnp.zeros((N, 2 * T), BF16)
    for r in range(R):
        partial[r, 0:N, :] = jnp.zeros((N, TILES * T), BF16)
        partial[r, (N + 1) * N:(N + 2) * N, :] = jnp.zeros((N, TILES * T), BF16)
    corner_s[...] = jnp.zeros_like(corner_s)

    def take(ref):
        parts = [ref[pl.ds(e * (N - 1), EDGE, stride=N), :] for e in range(2)]
        for e in range(2):
            for r in range(R):
                start = r * ROWS + e * (ROWS - N)
                parts.append(ref[start:start + N, :])
        return jnp.concatenate(parts, axis=0)

    def solve_edges(v):
        scale = jnp.concatenate([spread(admit_e[e * N:(e + 1) * N, :]) for e in range(4)], axis=0)
        near_e = jnp.concatenate([take(near_a), take(near_h)], axis=1)
        rest = (inc_e[...] - near_e).astype(BF16)
        cur_e = dot(rest[:, 0:U], solve[...]) * scale
        far_e = jnp.concatenate([take(far_a), take(far_h)], axis=1)
        back = ((src_e[...] - far_e) * scale).astype(BF16)
        adj_e = dot(back[:, 0:U], solve_t[...])

        for e in range(2):
            rows = slice(e * EDGE, (e + 1) * EDGE)
            corner_s[0, 0:EDGE, :] = cur_e[rows, 0:T]
            corner_s[1, 0:EDGE, :] = cur_e[rows, T:]
            corner_s[2, 0:EDGE, :] = adj_e[rows, 0:T]
            corner_s[3, 0:EDGE, :] = adj_e[rows, T:]
            cut = [
                jnp.concatenate([corner_s[k, pl.ds(0, 8, stride=N), :], corner_s[k, pl.ds(N - 1, 8, stride=N), :]], axis=0)
                for k in range(4)
            ]
            state = jnp.concatenate([adj_e[rows], jnp.concatenate(cut[2:], axis=1)], axis=0).astype(BF16)
            out = []
            for k, t in enumerate(Y_TILES[e]):
                gain_k = gains_y[e, :, k * T:(k + 1) * T]
                out.append(dot(state, weights_t[:, t * T:(t + 1) * T]) * spread(gain_k[0:N], gain_k[N:]))
            part_a = turn(out[0][:EDGE], -1) + out[1][:EDGE] + turn(out[2][:EDGE], 1)
            part_h = fold(
                jnp.where(low(EDGE), turn(out[3][:EDGE], -1), turn(out[3][:EDGE], 1)) + out[4][:EDGE]
            )
            tail_a = out[0][EDGE:] + out[1][EDGE:] + out[2][EDGE:]
            tail_h = fold(out[3][EDGE:] + out[4][EDGE:])
            message = jnp.concatenate(
                [cur_e[rows, 0:T], jnp.where(low(EDGE), cur_e[rows, T:], part_h), part_a], axis=1
            ).astype(BF16)
            send_y[v, e] = message.reshape(R, N, 3 * T)
            tail = jnp.concatenate([cut[0], jnp.where(low(N), cut[1], tail_h), tail_a], axis=1)
            send_c[v, 2 * e] = tail[0:8]
            send_c[v, 2 * e + 1] = tail[8:16]
        for e in range(2):
            rows = slice((2 + e) * EDGE, (3 + e) * EDGE)
            state = adj_e[rows].astype(BF16)
            out = []
            for k, t in enumerate(X_TILES[e]):
                out.append(dot(state, weights_t[:, t * T:(t + 1) * T]) * spread(gains_x[e, :, k * T:(k + 1) * T]))
            part_a = turn(out[0], -1) + out[1] + turn(out[2], 1)
            part_h = fold(turn(out[3], -1) + out[4] + turn(out[5], 1))
            message = jnp.concatenate(
                [cur_e[rows, 0:T], jnp.where(low(EDGE), cur_e[rows, T:], part_h), part_a], axis=1
            ).astype(BF16)
            send_x[v, e] = message.reshape(R, N, 3 * T)

    def copies(v):
        made = []
        for e in range(2):
            made.append((send_y.at[v, e], recv_y.at[v, 1 - e], y_to[e], e, 1 - e))
        for e in range(2):
            made.append((send_x.at[v, e], recv_x.at[v, 1 - e], x_to[e], 2 + e, 3 - e))
        for q in range(4):
            made.append((send_c.at[v, q], recv_c.at[v, 3 - q], c_to[q], 4 + q, 7 - q))
        return [
            pltpu.make_async_remote_copy(
                src_ref=a, dst_ref=b, send_sem=send_sem.at[v, s], recv_sem=recv_sem.at[v, t],
                device_id=where, device_id_type=MESH,
            )
            for a, b, where, s, t in made
        ]

    def right_sides(c):
        at = pl.ds(pl.multiple_of(c * MANY, MANY), MANY)
        near = jnp.concatenate([near_a[at, :], near_h[at, 0:HALF]], axis=1)
        far = jnp.concatenate([far_a[at, :], far_h[at, 0:HALF]], axis=1)
        rest = (inc[at, :].astype(F32) - near).astype(BF16)
        back = src[at, :].astype(F32) - far
        back = [back[k * ROWS:(k + 1) * ROWS] * admit[:, 0:U] for k in range(PER)]
        return rest, jnp.concatenate(back, axis=0).astype(BF16)

    def solve_chunk(c, carry):
        rest, back = right_sides(c)
        cur = dot(rest, solve[...])
        for k in range(PER):
            r = c * PER + k
            one_cur = cur[k * ROWS:(k + 1) * ROWS] * admit[...]
            v0[r, N:N + ROWS, :] = one_cur.astype(BF16)
            vm[r, N:N + ROWS, :] = turn(one_cur, 1).astype(BF16)
            vp[r, N:N + ROWS, :] = turn(one_cur, -1).astype(BF16)
        at = pl.ds(pl.multiple_of(c * MANY, MANY), MANY)
        adj[at, :] = dot(back, solve_t[...]).astype(BF16)
        return carry

    shifted = {-1: vm, 0: v0, 1: vp}

    def product_chunk(c, carry):
        at = pl.ds(pl.multiple_of(c * MANY, MANY), MANY)
        state = adj[at, :]
        for t in range(TILES // 2):
            columns = slice(2 * t * T, 2 * (t + 1) * T)
            value = dot(state, weights_t[:, columns]).astype(BF16)
            for k in range(PER):
                partial[c * PER + k, N:N + ROWS, columns] = value[k * ROWS:(k + 1) * ROWS] * gains[:, columns]
        for k in range(PER):
            r = c * PER + k
            rows = pl.ds(pl.multiple_of(r * ROWS, ROWS), ROWS)

            def nearby(d, columns):
                sx, sy = STEPS[d]
                return shifted[sy][r, N * (1 + sx):N * (1 + sx) + ROWS, columns]

            for d in range(8):
                columns = slice(d * T, (d + 1) * T)
                lhs[rows, columns] = nearby(d, slice(0, T)) * gains[:, columns]
            for p, (d0, d1) in enumerate(PAIRS):
                columns = slice((8 + p) * T, (9 + p) * T)
                both = jnp.where(low(ROWS), nearby(d0, slice(T, 2 * T)), nearby(d1, slice(T, 2 * T)))
                lhs[rows, columns] = both * gains[:, columns]
        return carry

    def sum_chunk(c, carry):
        at = pl.ds(pl.multiple_of(c * MANY, MANY), MANY)
        near = dot(lhs[at, :], weights[...])
        near_a[at, :] = near[:, 0:T]
        near_h[at, :] = near[:, T:]
        for k in range(PER):
            r = c * PER + k

            def part(x, t):
                return partial[r, x * N:(x + 1) * N, t * T:(t + 1) * T].astype(F32)

            for x in range(N):
                sums = {sy: None for sy in (-1, 0, 1)}
                for d, (sx, sy) in enumerate(STEPS):
                    value = part(1 + x - sx, d)
                    sums[sy] = value if sums[sy] is None else sums[sy] + value
                a = turn(sums[1], 1) + sums[0] + turn(sums[-1], -1)
                tops = {sy: jnp.where(low(N), part(2 + x, 9 + sy), part(x, 9 + sy)) for sy in (-1, 0, 1)}
                mid = part(1 + x, 11)
                below = tops[-1] + jnp.where(low(N), mid, 0.0)
                above = tops[1] + jnp.where(low(N), 0.0, mid)
                h = fold(turn(above, 1) + tops[0] + turn(below, -1))
                rows = pl.ds(pl.multiple_of(r * ROWS + x * N, N), N)
                far_a[rows, :] = a
                far_h[rows, :] = h
        return carry

    def correct(v):
        for e in range(2):
            whole = jnp.concatenate(
                [recv_y[v, e].reshape(EDGE, 3 * T).astype(F32), recv_c[v, 2 * e], recv_c[v, 2 * e + 1]], axis=0
            )
            rows = EDGE + N
            a, mixed, part_a = whole[:, 0:T], whole[:, T:2 * T], whole[:, 2 * T:]
            other = turn(mixed, HALF, 1)
            h = jnp.where(low(rows), mixed, other)

            def moved(x, j):
                return jnp.concatenate([turn(x[:EDGE], -j), x[EDGE:]], axis=0)

            tiles = [moved(a, -1), a, moved(a, 1), jnp.where(low(rows), moved(h, -1), moved(h, 1)), h]
            scaled = []
            for k, tile in enumerate(tiles):
                gain_k = gains_y[e, :, k * T:(k + 1) * T]
                scaled.append((tile * spread(gain_k[0:N], gain_k[N:])).astype(BF16))
            matrix = jnp.concatenate([weights[t * T:(t + 1) * T, :] for t in Y_TILES[e]], axis=0)
            extra = dot(jnp.concatenate(scaled, axis=1), matrix)
            for ref, value in (
                (near_a, extra[:, 0:T]), (near_h, extra[:, T:]), (far_a, part_a), (far_h, other)
            ):
                y0 = e * (N - 1)
                for at, piece in (
                    (pl.ds(y0, EDGE, stride=N), value[:EDGE]),
                    (pl.ds(y0, 8, stride=ROWS), value[EDGE:EDGE + 8]),
                    (pl.ds(y0 + ROWS - N, 8, stride=ROWS), value[EDGE + 8:]),
                ):
                    ref[at, :] = ref[at, :] + piece
        for e in range(2):
            whole = recv_x[v, e].reshape(EDGE, 3 * T).astype(F32)
            a, mixed, part_a = whole[:, 0:T], whole[:, T:2 * T], whole[:, 2 * T:]
            other = turn(mixed, HALF, 1)
            h = mixed if e == 0 else other
            tiles = [turn(a, 1), a, turn(a, -1), turn(h, 1), h, turn(h, -1)]
            scaled = []
            for k, tile in enumerate(tiles):
                scaled.append((tile * spread(gains_x[e, :, k * T:(k + 1) * T])).astype(BF16))
            matrix = jnp.concatenate([weights[t * T:(t + 1) * T, :] for t in X_TILES[e]], axis=0)
            extra = dot(jnp.concatenate(scaled, axis=1), matrix)
            for ref, value in (
                (near_a, extra[:, 0:T]), (near_h, extra[:, T:]), (far_a, part_a), (far_h, other)
            ):
                for r in range(R):
                    start = r * ROWS + e * (ROWS - N)
                    ref[start:start + N, :] = ref[start:start + N, :] + value[r * N:(r + 1) * N]

    pl.semaphore_wait(barrier, 8)

    def sweep(v, carry):
        solve_edges(v)
        for copy in copies(v):
            copy.start()
        lax.fori_loop(0, R // PER, solve_chunk, 0)
        lax.fori_loop(0, R // PER, product_chunk, 0)
        lax.fori_loop(0, R // PER, sum_chunk, 0)
        for copy in copies(v):
            copy.wait_recv()
        correct(v)
        for copy in copies(v):
            copy.wait_send()
        return carry

    lax.fori_loop(0, SWEEPS, sweep, 0)

    def finish(c, carry):
        rest, back = right_sides(c)
        cur = dot(rest, solve[:, 0:U])
        for k in range(PER):
            cur_out[c * PER + k] = (cur[k * ROWS:(k + 1) * ROWS] * admit[:, 0:U]).astype(BF16)
        value = dot(back, solve_tn[...]).astype(BF16)
        for k in range(PER):
            adj_out[c * PER + k] = value[k * ROWS:(k + 1) * ROWS]
        return carry

    lax.fori_loop(0, R // PER, finish, 0)


def solution(mesh):
    nx, ny = mesh.shape["gx"], mesh.shape["gy"]

    def local(inc, src, cls, slot, gain, adm, coup, sinv):
        vmem = pl.BlockSpec(memory_space=pltpu.VMEM)
        out = jax.ShapeDtypeStruct((R, ROWS, U), BF16)
        cur, adj = pl.pallas_call(
            functools.partial(kernel, nx, ny),
            out_shape=(out, out),
            in_specs=[vmem] * 8,
            out_specs=(vmem, vmem),
            scratch_shapes=[
                pltpu.VMEM((R, ROWS + 2 * N, 2 * T), BF16),
                pltpu.VMEM((R, ROWS + 2 * N, 2 * T), BF16),
                pltpu.VMEM((R, ROWS + 2 * N, 2 * T), BF16),
                pltpu.VMEM((R * ROWS, 2 * T), BF16),
                pltpu.VMEM((8 * ROWS, T), F32),
                pltpu.VMEM((8 * ROWS, T), F32),
                pltpu.VMEM((8 * ROWS, T), F32),
                pltpu.VMEM((8 * ROWS, T), F32),
                pltpu.VMEM((ROWS, TILES * T), BF16),
                pltpu.VMEM((R * ROWS, TILES * T), BF16),
                pltpu.VMEM((TILES * T, 2 * T), BF16),
                pltpu.VMEM((2 * T, TILES * T), BF16),
                pltpu.VMEM((R, ROWS + 2 * N, TILES * T), BF16),
                pltpu.VMEM((ROWS, 2 * T), F32),
                pltpu.VMEM((4 * N, 2 * T), F32),
                pltpu.VMEM((4 * EDGE, 2 * T), F32),
                pltpu.VMEM((4 * EDGE, 2 * T), F32),
                pltpu.VMEM((2, 2 * N, 5 * T), F32),
                pltpu.VMEM((2, N, 6 * T), F32),
                pltpu.VMEM((U, 2 * T), BF16),
                pltpu.VMEM((U, 2 * T), BF16),
                pltpu.VMEM((U, U), BF16),
                pltpu.VMEM((4, 8 * N, T), F32),
                pltpu.VMEM((SWEEPS, 2, R, N, 3 * T), BF16),
                pltpu.VMEM((SWEEPS, 2, R, N, 3 * T), BF16),
                pltpu.VMEM((SWEEPS, 4, 8, 3 * T), F32),
                pltpu.VMEM((SWEEPS, 2, R, N, 3 * T), BF16),
                pltpu.VMEM((SWEEPS, 2, R, N, 3 * T), BF16),
                pltpu.VMEM((SWEEPS, 4, 8, 3 * T), F32),
                pltpu.SemaphoreType.DMA((SWEEPS, 8)),
                pltpu.SemaphoreType.DMA((SWEEPS, 8)),
            ],
            compiler_params=pltpu.CompilerParams(
                collective_id=0, has_side_effects=True, vmem_limit_bytes=60 * 1024 * 1024
            ),
        )(
            inc.reshape(R * ROWS, U), src.reshape(R * ROWS, U), cls, slot, gain.reshape(64, U), adm, coup, sinv
        )
        return cur.reshape(R, N, N, U), adj.reshape(R, N, N, U)

    placed = (P(None, "gx", "gy", None), P(None, "gx", "gy", None), P("gx", "gy"), P(), P(), P(), P(), P())
    return jax.shard_map(
        local, mesh=mesh, in_specs=placed, out_specs=(placed[0], placed[0]), check_vma=False
    )
```

```python
import functools

import jax
import jax.numpy as jnp
from jax import lax
from jax.experimental import pallas as pl
from jax.experimental.pallas import tpu as pltpu
from jax.sharding import PartitionSpec as P

MESH = pl.DeviceIdType.MESH
F32 = jnp.float32
BF16 = jnp.bfloat16
SWEEPS = 3
R = 6
N = 16
ROWS = N * N
EDGE = R * N
U = 192
MANY = R * ROWS
T = 128
HALF = 64
STEPS = ((-1, -1), (-1, 0), (-1, 1), (0, -1), (0, 1), (1, -1), (1, 0), (1, 1))
PAIRS = ((0, 5), (1, 6), (2, 7), (3, 4))
TILES = 12
Y_DIRS = ((0, 3, 5), (2, 4, 7))
X_DIRS = ((0, 1, 2), (5, 6, 7))
Y_TILES = ((0, 3, 5, 8, 11), (2, 4, 7, 10, 11))
X_TILES = ((0, 1, 2, 8, 9, 10), (5, 6, 7, 8, 9, 10))


def dot(a, b):
    return jnp.dot(a, b, preferred_element_type=F32)


def dot_nt(a, b):
    return lax.dot_general(a, b, (((1,), (1,)), ((), ())), preferred_element_type=F32)


def iota(shape, dim):
    return lax.broadcasted_iota(jnp.int32, shape, dim)


def low(rows):
    return iota((rows, T), 1) < HALF


def turn(x, shift, axis=0):
    size = x.shape[axis]
    return x if shift % size == 0 else pltpu.roll(x, shift % size, axis)


def spread(tile, corner=None):
    return jnp.concatenate([tile] * R + ([] if corner is None else [corner]), axis=0)


def fold(tile):
    return tile + turn(tile, HALF, 1)


def pack(a, h):
    half = EDGE // 2
    return jnp.concatenate([a, jnp.where(low(half), h[:half], h[half:])], axis=0).astype(BF16)


def unpack(message):
    value = message.astype(F32)
    mixed = value[EDGE:]
    other = turn(mixed, HALF, 1)
    keep = low(EDGE // 2)
    return value[:EDGE], jnp.concatenate([jnp.where(keep, mixed, other), jnp.where(keep, other, mixed)], axis=0)


def kernel(
    nx, ny,
    inc_hbm, src_hbm, cls, slot, gain, adm, coup_hbm, sinv,
    rest_out, back_out, admit_out,
    inc, src, coup, load_sem,
    v0, vm, vp, adj, near_a, near_h, far_a, far_h, gains, lhs, weights, weights_t, partial,
    admit, admit_e, inc_e, src_e, gains_y, gains_x, solve, solve_t, corner_s,
    send_y, send_x, send_c, recv_y, recv_x, recv_c,
    send_sem, recv_sem,
):
    gx, gy = lax.axis_index("gx"), lax.axis_index("gy")
    left, right = lax.rem(gx + nx - 1, nx), lax.rem(gx + 1, nx)
    down, up = lax.rem(gy + ny - 1, ny), lax.rem(gy + 1, ny)
    y_to = ((gx, down), (gx, up))
    x_to = ((left, gy), (right, gy))
    c_to = ((left, down), (right, down), (left, up), (right, up))

    barrier = pltpu.get_barrier_semaphore()
    for where in y_to + x_to + c_to:
        pl.semaphore_signal(barrier, inc=1, device_id=where, device_id_type=MESH)

    loads = [
        pltpu.make_async_copy(a, b, load_sem.at[k])
        for k, (a, b) in enumerate(((inc_hbm, inc), (coup_hbm, coup), (src_hbm, src)))
    ]
    stores = [
        pltpu.make_async_copy(a, b, load_sem.at[3 + k])
        for k, (a, b) in enumerate(((inc, rest_out), (src, back_out), (admit, admit_out)))
    ]
    for load in loads:
        load.start()

    def take(ref):
        parts = [ref[pl.ds(e * (N - 1), EDGE, stride=N), :] for e in range(2)]
        for e in range(2):
            for r in range(R):
                start = r * ROWS + e * (ROWS - N)
                parts.append(ref[start:start + N, :])
        return jnp.concatenate(parts, axis=0)

    def edge_rows(data, a_ref, h_ref, e_ref):
        h_ref[...] = jnp.zeros_like(h_ref)
        for r in range(R):
            a_ref[r * ROWS:(r + 1) * ROWS, :] = data[r * ROWS:(r + 1) * ROWS, 0:T].astype(F32)
            h_ref[r * ROWS:(r + 1) * ROWS, 0:HALF] = data[r * ROWS:(r + 1) * ROWS, T:U].astype(F32)
        for k, ref in enumerate((a_ref, h_ref)):
            columns = slice(k * T, (k + 1) * T)
            e_ref[:, columns] = take(ref)
            ref[...] = jnp.zeros_like(ref)

    def scale_e():
        return jnp.concatenate([spread(admit_e[e * N:(e + 1) * N, :]) for e in range(4)], axis=0)

    def corners(k, value):
        corner_s[k, 0:EDGE, :] = value
        return jnp.concatenate([corner_s[k, pl.ds(0, 8, stride=N), :], corner_s[k, pl.ds(N - 1, 8, stride=N), :]], axis=0)

    def edges_f(v):
        near_e = jnp.concatenate([take(near_a), take(near_h)], axis=1)
        rest = (inc_e[...] - near_e).astype(BF16)
        cur_e = dot(rest[:, 0:U], solve[...]) * scale_e()
        for e in range(2):
            rows = slice(e * EDGE, (e + 1) * EDGE)
            send_y[0, v, e] = pack(cur_e[rows, 0:T], cur_e[rows, T:])
            both = jnp.concatenate([corners(2 * e, cur_e[rows, 0:T]), corners(2 * e + 1, cur_e[rows, T:])], axis=1)
            send_c[0, v, 2 * e] = both[0:8]
            send_c[0, v, 2 * e + 1] = both[8:16]
        for e in range(2):
            rows = slice((2 + e) * EDGE, (3 + e) * EDGE)
            send_x[0, v, e] = pack(cur_e[rows, 0:T], cur_e[rows, T:])

    def edges_a(v):
        far_e = jnp.concatenate([take(far_a), take(far_h)], axis=1)
        back = ((src_e[...] - far_e) * scale_e()).astype(BF16)
        adj_e = dot(back[:, 0:U], solve_t[...])
        for e in range(2):
            rows = slice(e * EDGE, (e + 1) * EDGE)
            cut = [corners(4 + 2 * e + k, adj_e[rows, k * T:(k + 1) * T]) for k in range(2)]
            state = jnp.concatenate([adj_e[rows], jnp.concatenate(cut, axis=1)], axis=0).astype(BF16)
            out = []
            for k, t in enumerate(Y_TILES[e]):
                gain_k = gains_y[e, :, k * T:(k + 1) * T]
                out.append(dot(state, weights_t[:, t * T:(t + 1) * T]) * spread(gain_k[0:N], gain_k[N:]))
            part_a = turn(out[0][:EDGE], -1) + out[1][:EDGE] + turn(out[2][:EDGE], 1)
            part_h = fold(
                jnp.where(low(EDGE), turn(out[3][:EDGE], -1), turn(out[3][:EDGE], 1)) + out[4][:EDGE]
            )
            tail_a = out[0][EDGE:] + out[1][EDGE:] + out[2][EDGE:]
            tail_h = fold(out[3][EDGE:] + out[4][EDGE:])
            send_y[1, v, e] = pack(part_a, part_h)
            tail = jnp.concatenate([tail_a, tail_h], axis=1)
            send_c[1, v, 2 * e] = tail[0:8]
            send_c[1, v, 2 * e + 1] = tail[8:16]
        for e in range(2):
            state = adj_e[(2 + e) * EDGE:(3 + e) * EDGE].astype(BF16)
            out = []
            for k, t in enumerate(X_TILES[e]):
                out.append(dot(state, weights_t[:, t * T:(t + 1) * T]) * spread(gains_x[e, :, k * T:(k + 1) * T]))
            part_a = turn(out[0], -1) + out[1] + turn(out[2], 1)
            part_h = fold(turn(out[3], -1) + out[4] + turn(out[5], 1))
            send_x[1, v, e] = pack(part_a, part_h)

    inside_y = (gy > 0, gy < ny - 1)
    inside_x = (gx > 0, gx < nx - 1)

    def copies(kind, v):
        made = []
        for e in range(2):
            made.append((send_y.at[kind, v, e], recv_y.at[kind, v, 1 - e], y_to[e], e, 1 - e, inside_y[e], inside_y[1 - e]))
        for e in range(2):
            made.append((send_x.at[kind, v, e], recv_x.at[kind, v, 1 - e], x_to[e], 2 + e, 3 - e, inside_x[e], inside_x[1 - e]))
        for q in range(4):
            goes = inside_y[q // 2] & inside_x[q % 2]
            comes = inside_y[1 - q // 2] & inside_x[1 - q % 2]
            made.append((send_c.at[kind, v, q], recv_c.at[kind, v, 3 - q], c_to[q], 4 + q, 7 - q, goes, comes))
        return [
            (
                pltpu.make_async_remote_copy(
                    src_ref=a, dst_ref=b, send_sem=send_sem.at[kind, v, s], recv_sem=recv_sem.at[kind, v, t],
                    device_id=where, device_id_type=MESH,
                ),
                goes,
                comes,
            )
            for a, b, where, s, t, goes, comes in made
        ]

    def start(kind, v):
        for copy, goes, _ in copies(kind, v):
            pl.when(goes)(copy.start)

    def arrive(kind, v):
        for copy, _, comes in copies(kind, v):
            pl.when(comes)(copy.wait_recv)

    def sent(kind, v):
        for copy, goes, _ in copies(kind, v):
            pl.when(goes)(copy.wait_send)

    def no_sender():
        def clear(ref, q):
            for kind in range(2):
                for v in range(SWEEPS):
                    ref[kind, v, q] = jnp.zeros(ref.shape[3:], ref.dtype)

        for e in range(2):
            pl.when(jnp.logical_not(inside_y[e]))(functools.partial(clear, recv_y, e))
            pl.when(jnp.logical_not(inside_x[e]))(functools.partial(clear, recv_x, e))
        for q in range(4):
            pl.when(jnp.logical_not(inside_y[q // 2] & inside_x[q % 2]))(functools.partial(clear, recv_c, q))

    def right_f():
        near = jnp.concatenate([near_a[0:MANY, :], near_h[0:MANY, 0:HALF]], axis=1)
        return (inc[...].astype(F32) - near).astype(BF16)

    def right_a():
        far = jnp.concatenate([far_a[0:MANY, :], far_h[0:MANY, 0:HALF]], axis=1)
        back = src[...].astype(F32) - far
        back = [back[r * ROWS:(r + 1) * ROWS] * admit[:, 0:U] for r in range(R)]
        return jnp.concatenate(back, axis=0).astype(BF16)

    shifted = {-1: vm, 0: v0, 1: vp}

    def main_f():
        cur = dot(right_f(), solve[...])
        for r in range(R):
            one_cur = cur[r * ROWS:(r + 1) * ROWS] * admit[...]
            v0[r, N:N + ROWS, :] = one_cur.astype(BF16)
            vm[r, N:N + ROWS, :] = turn(one_cur, 1).astype(BF16)
            vp[r, N:N + ROWS, :] = turn(one_cur, -1).astype(BF16)
        for r in range(R):
            rows = slice(r * ROWS, (r + 1) * ROWS)

            def nearby(d, columns):
                sx, sy = STEPS[d]
                return shifted[sy][r, N * (1 + sx):N * (1 + sx) + ROWS, columns]

            for d in range(8):
                columns = slice(d * T, (d + 1) * T)
                lhs[rows, columns] = nearby(d, slice(0, T)) * gains[:, columns]
            for p, (d0, d1) in enumerate(PAIRS):
                columns = slice((8 + p) * T, (9 + p) * T)
                both = jnp.where(low(ROWS), nearby(d0, slice(T, 2 * T)), nearby(d1, slice(T, 2 * T)))
                lhs[rows, columns] = both * gains[:, columns]
        near = dot(lhs[...], weights[...])
        near_a[0:MANY, :] = near[:, 0:T]
        near_h[0:MANY, :] = near[:, T:]

    def main_a():
        adj[...] = dot(right_a(), solve_t[...]).astype(BF16)
        for t in range(TILES // 2):
            columns = slice(2 * t * T, 2 * (t + 1) * T)
            value = dot(adj[...], weights_t[:, columns]).astype(BF16)
            for r in range(R):
                partial[r, N:N + ROWS, columns] = value[r * ROWS:(r + 1) * ROWS] * gains[:, columns]
        for r in range(R):

            def part(x, t):
                return partial[r, x * N:(x + 1) * N, t * T:(t + 1) * T].astype(F32)

            for x in range(N):
                sums = {sy: None for sy in (-1, 0, 1)}
                for d, (sx, sy) in enumerate(STEPS):
                    value = part(1 + x - sx, d)
                    sums[sy] = value if sums[sy] is None else sums[sy] + value
                a = turn(sums[1], 1) + sums[0] + turn(sums[-1], -1)
                tops = {sy: jnp.where(low(N), part(2 + x, 9 + sy), part(x, 9 + sy)) for sy in (-1, 0, 1)}
                mid = part(1 + x, 11)
                below = tops[-1] + jnp.where(low(N), mid, 0.0)
                above = tops[1] + jnp.where(low(N), 0.0, mid)
                h = fold(turn(above, 1) + tops[0] + turn(below, -1))
                at = r * ROWS + x * N
                far_a[at:at + N, :] = a
                far_h[at:at + N, :] = h

    def add_y(e, ref, value, tail):
        y0 = e * (N - 1)
        for at, piece in (
            (pl.ds(y0, EDGE, stride=N), value),
            (pl.ds(y0, 8, stride=ROWS), tail[0:8]),
            (pl.ds(y0 + ROWS - N, 8, stride=ROWS), tail[8:16]),
        ):
            ref[at, :] = ref[at, :] + piece

    def add_x(e, ref, value):
        for r in range(R):
            at = r * ROWS + e * (ROWS - N)
            ref[at:at + N, :] = ref[at:at + N, :] + value[r * N:(r + 1) * N]

    def correct_f(v):
        for e in range(2):
            a, h = unpack(recv_y[0, v, e])
            tail = jnp.concatenate([recv_c[0, v, 2 * e], recv_c[0, v, 2 * e + 1]], axis=0)
            tail_a, tail_h = tail[:, 0:T], tail[:, T:]
            tiles = [
                (turn(a, 1), tail_a), (a, tail_a), (turn(a, -1), tail_a),
                (jnp.where(low(EDGE), turn(h, 1), turn(h, -1)), tail_h), (h, tail_h),
            ]
            scaled = []
            for k, tile in enumerate(tiles):
                gain_k = gains_y[e, :, k * T:(k + 1) * T]
                scaled.append((jnp.concatenate(tile, axis=0) * spread(gain_k[0:N], gain_k[N:])).astype(BF16))
            matrix = jnp.concatenate([weights[t * T:(t + 1) * T, :] for t in Y_TILES[e]], axis=0)
            extra = dot(jnp.concatenate(scaled, axis=1), matrix)
            add_y(e, near_a, extra[:EDGE, 0:T], extra[EDGE:, 0:T])
            add_y(e, near_h, extra[:EDGE, T:], extra[EDGE:, T:])
        for e in range(2):
            a, h = unpack(recv_x[0, v, e])
            tiles = [turn(a, 1), a, turn(a, -1), turn(h, 1), h, turn(h, -1)]
            scaled = []
            for k, tile in enumerate(tiles):
                scaled.append((tile * spread(gains_x[e, :, k * T:(k + 1) * T])).astype(BF16))
            matrix = jnp.concatenate([weights[t * T:(t + 1) * T, :] for t in X_TILES[e]], axis=0)
            extra = dot(jnp.concatenate(scaled, axis=1), matrix)
            add_x(e, near_a, extra[:, 0:T])
            add_x(e, near_h, extra[:, T:])

    def correct_a(v):
        for e in range(2):
            a, h = unpack(recv_y[1, v, e])
            tail = jnp.concatenate([recv_c[1, v, 2 * e], recv_c[1, v, 2 * e + 1]], axis=0)
            add_y(e, far_a, a, tail[:, 0:T])
            add_y(e, far_h, h, tail[:, T:])
        for e in range(2):
            a, h = unpack(recv_x[1, v, e])
            add_x(e, far_a, a)
            add_x(e, far_h, h)

    one = jnp.float32(1.0)
    has_left, has_right = jnp.where(gx > 0, 1.0, 0.0) * one, jnp.where(gx < nx - 1, 1.0, 0.0) * one
    has_down, has_up = jnp.where(gy > 0, 1.0, 0.0) * one, jnp.where(gy < ny - 1, 1.0, 0.0) * one

    def chooser(rows, columns, wanted):
        return jnp.where(iota((rows, columns), 0) == wanted, 1.0, 0.0).astype(BF16)

    lane = iota((U, 2 * T), 1)
    dup = chooser(U, 2 * T, jnp.where(lane < U, lane, lane - HALF))
    dup_back = chooser(U, 2 * T, jnp.where(lane < HALF, lane + T, jnp.where(lane < T, lane + HALF, lane - T)))
    eye = chooser(U, U, iota((U, U), 1))
    solve[...] = dot(sinv[...], dup).astype(BF16)
    solve_n = dot_nt(eye, sinv[...]).astype(BF16)
    solve_t[...] = dot(solve_n, dup_back).astype(BF16)

    adm_high = adm[...].astype(BF16).astype(F32)
    adm_both = jnp.concatenate([adm_high, adm[...] - adm_high], axis=0).astype(BF16)
    adm_table = dot(adm_both, dup).astype(BF16)

    diag = iota((N, N), 0) == iota((N, N), 1)
    spots = [jnp.where(diag, cls[x:x + 1, :].astype(F32), 0.0) for x in range(N)]
    kind = dot(jnp.concatenate(spots, axis=0).astype(BF16), jnp.ones((N, N), BF16))

    def onehot(kinds):
        which = lax.rem(iota((kinds.shape[0], N), 1), 8)
        return jnp.where(which.astype(F32) == kinds, 1.0, 0.0).astype(BF16)

    kind_e = jnp.concatenate(
        [
            jnp.broadcast_to(cls[:, 0:1].astype(F32), (N, N)),
            jnp.broadcast_to(cls[:, N - 1:N].astype(F32), (N, N)),
            kind[0:N],
            kind[ROWS - N:ROWS],
        ],
        axis=0,
    )
    hot, hot_e = onehot(kind), onehot(kind_e)
    admit_e[...] = dot(hot_e, adm_table)
    corner_s[...] = jnp.zeros_like(corner_s)
    no_sender()
    loads[0].wait()
    edge_rows(inc, near_a, near_h, inc_e)
    pick = [
        jnp.where(iota((8, 64), 1) == iota((8, 64), 0) * 8 + slot[:, d:d + 1], 1.0, 0.0)
        for d in range(8)
    ]
    pick = jnp.concatenate(pick, axis=0).astype(BF16)
    gain_dup = dot(gain[...].astype(BF16), dup).astype(BF16)
    table64 = dot(pick, gain_dup)
    pieces = [table64[d * 8:(d + 1) * 8, 0:T] for d in range(8)]
    for d0, d1 in PAIRS:
        pieces.append(jnp.where(low(8), table64[d0 * 8:(d0 + 1) * 8, T:], table64[d1 * 8:(d1 + 1) * 8, T:]))
    table = jnp.concatenate(pieces, axis=1)
    table = jnp.concatenate([table, jnp.zeros_like(table)], axis=0).astype(BF16)
    edge_gain = dot(hot_e, table)
    spot = iota((N, T), 0)

    def along(j):
        return jnp.where((spot + j >= 0) & (spot + j < N), 1.0, 0.0)

    lows = jnp.where(low(N), 1.0, 0.0)
    for e, exists in enumerate((has_down, has_up)):
        raw = edge_gain[e * N:(e + 1) * N]
        first = jnp.where(spot < 8, 1.0, 0.0)
        side = first * has_left + (1.0 - first) * has_right
        for k, t in enumerate(Y_TILES[e]):
            tile = raw[:, t * T:(t + 1) * T]
            ends = jnp.where(spot < 8, jnp.broadcast_to(tile[0:1], (N, T)), jnp.broadcast_to(tile[N - 1:N], (N, T)))
            if k < 3:
                keep = along(k - 1)
                corner = (first, 0.0 * first, 1.0 - first)[k]
            elif k == 3:
                keep = lows * along(-1) + (1.0 - lows) * along(1)
                corner = lows * first + (1.0 - lows) * (1.0 - first)
            else:
                keep = lows if e == 0 else 1.0 - lows
                corner = 0.0 * first
            gains_y[e, 0:N, k * T:(k + 1) * T] = tile * keep * exists
            gains_y[e, N:2 * N, k * T:(k + 1) * T] = ends * corner * side * exists
    for e, exists in enumerate((has_left, has_right)):
        raw = edge_gain[(2 + e) * N:(3 + e) * N]
        for k, t in enumerate(X_TILES[e]):
            keep = along(k % 3 - 1)
            if k >= 3:
                keep = keep * (lows if e == 0 else 1.0 - lows)
            gains_x[e, :, k * T:(k + 1) * T] = raw[:, t * T:(t + 1) * T] * keep * exists

    loads[1].wait()
    weights[...] = jnp.zeros_like(weights)
    for d in range(8):
        weights[d * T:(d + 1) * T, 0:U] = coup[d, 0:T, :]
    for p, (d0, d1) in enumerate(PAIRS):
        base = (8 + p) * T
        weights[base:base + HALF, 0:U] = coup[d0, T:U, :]
        weights[base + HALF:base + T, 0:U] = coup[d1, T:U, :]
    row = iota((2 * T, U), 0)
    place = jnp.where(row < HALF, -1, jnp.where(row < T, row + HALF, row - T))
    order = jnp.where(iota((2 * T, U), 1) == place, 1.0, 0.0).astype(BF16)
    for t in range(TILES):
        weights_t[:, t * T:(t + 1) * T] = dot_nt(order, weights[t * T:(t + 1) * T, 0:U]).astype(BF16)

    loads[2].wait()
    edge_rows(src, far_a, far_h, src_e)

    admit[...] = dot(hot, adm_table)
    stores[2].start()

    def inside(rows, sx, sy):
        r = iota((rows, T), 0)
        x, y = r // N + sx, lax.rem(r, N) + sy
        return (x >= 0) & (x < N) & (y >= 0) & (y < N)

    for t in range(TILES):
        value = dot(hot, table[:, t * T:(t + 1) * T])
        if t < 8:
            keep = jnp.where(inside(ROWS, *STEPS[t]), 1.0, 0.0)
        else:
            d0, d1 = PAIRS[t - 8]
            keep = jnp.where(
                low(ROWS), jnp.where(inside(ROWS, *STEPS[d0]), 1.0, 0.0), jnp.where(inside(ROWS, *STEPS[d1]), 1.0, 0.0)
            )
        gains[:, t * T:(t + 1) * T] = (value * keep).astype(BF16)

    for ref in (v0, vm, vp):
        for r in range(R):
            ref[r, 0:N, :] = jnp.zeros((N, 2 * T), BF16)
            ref[r, (N + 1) * N:(N + 2) * N, :] = jnp.zeros((N, 2 * T), BF16)
    for r in range(R):
        partial[r, 0:N, :] = jnp.zeros((N, TILES * T), BF16)
        partial[r, (N + 1) * N:(N + 2) * N, :] = jnp.zeros((N, TILES * T), BF16)

    edges_f(0)
    edges_a(0)
    pl.semaphore_wait(barrier, 8)
    start(0, 0)
    start(1, 0)
    main_f()

    def sweep(v, carry):
        main_a()
        arrive(0, v)
        correct_f(v)
        edges_f(v + 1)
        start(0, v + 1)
        main_f()
        arrive(1, v)
        correct_a(v)
        edges_a(v + 1)
        start(1, v + 1)
        return carry

    lax.fori_loop(0, SWEEPS - 1, sweep, 0)
    main_a()
    arrive(0, SWEEPS - 1)
    correct_f(SWEEPS - 1)
    inc[...] = right_f()
    stores[0].start()
    arrive(1, SWEEPS - 1)
    correct_a(SWEEPS - 1)
    src[...] = right_a()
    stores[1].start()
    for kind in range(2):
        for v in range(SWEEPS):
            sent(kind, v)
    for store in stores:
        store.wait()


def last(rest, back, admit, sinv, cur_out, adj_out):
    cur = dot(rest[...], sinv[...])
    for r in range(R // 2):
        rows = slice(r * ROWS, (r + 1) * ROWS)
        cur_out[rows, :] = (cur[rows] * admit[:, 0:U]).astype(BF16)
    adj_out[...] = dot_nt(back[...], sinv[...]).astype(BF16)


def solution(mesh):
    nx, ny = mesh.shape["gx"], mesh.shape["gy"]

    def local(inc, src, cls, slot, gain, adm, coup, sinv):
        vmem = pl.BlockSpec(memory_space=pltpu.VMEM)
        anywhere = pl.BlockSpec(memory_space=pl.ANY)
        out = jax.ShapeDtypeStruct((R * ROWS, U), BF16)
        rest, back, admit = pl.pallas_call(
            functools.partial(kernel, nx, ny),
            out_shape=(out, out, jax.ShapeDtypeStruct((ROWS, 2 * T), F32)),
            in_specs=[anywhere, anywhere, vmem, vmem, vmem, vmem, anywhere, vmem],
            out_specs=(anywhere, anywhere, anywhere),
            scratch_shapes=[
                pltpu.VMEM((R * ROWS, U), BF16),
                pltpu.VMEM((R * ROWS, U), BF16),
                pltpu.VMEM((8, U, U), BF16),
                pltpu.SemaphoreType.DMA((6,)),
                pltpu.VMEM((R, ROWS + 2 * N, 2 * T), BF16),
                pltpu.VMEM((R, ROWS + 2 * N, 2 * T), BF16),
                pltpu.VMEM((R, ROWS + 2 * N, 2 * T), BF16),
                pltpu.VMEM((R * ROWS, 2 * T), BF16),
                pltpu.VMEM((8 * ROWS, T), F32),
                pltpu.VMEM((8 * ROWS, T), F32),
                pltpu.VMEM((8 * ROWS, T), F32),
                pltpu.VMEM((8 * ROWS, T), F32),
                pltpu.VMEM((ROWS, TILES * T), BF16),
                pltpu.VMEM((R * ROWS, TILES * T), BF16),
                pltpu.VMEM((TILES * T, 2 * T), BF16),
                pltpu.VMEM((2 * T, TILES * T), BF16),
                pltpu.VMEM((R, ROWS + 2 * N, TILES * T), BF16),
                pltpu.VMEM((ROWS, 2 * T), F32),
                pltpu.VMEM((4 * N, 2 * T), F32),
                pltpu.VMEM((4 * EDGE, 2 * T), F32),
                pltpu.VMEM((4 * EDGE, 2 * T), F32),
                pltpu.VMEM((2, 2 * N, 5 * T), F32),
                pltpu.VMEM((2, N, 6 * T), F32),
                pltpu.VMEM((U, 2 * T), BF16),
                pltpu.VMEM((U, 2 * T), BF16),
                pltpu.VMEM((8, 8 * N, T), F32),
                pltpu.VMEM((2, SWEEPS, 2, EDGE + EDGE // 2, T), BF16),
                pltpu.VMEM((2, SWEEPS, 2, EDGE + EDGE // 2, T), BF16),
                pltpu.VMEM((2, SWEEPS, 4, 8, 2 * T), F32),
                pltpu.VMEM((2, SWEEPS, 2, EDGE + EDGE // 2, T), BF16),
                pltpu.VMEM((2, SWEEPS, 2, EDGE + EDGE // 2, T), BF16),
                pltpu.VMEM((2, SWEEPS, 4, 8, 2 * T), F32),
                pltpu.SemaphoreType.DMA((2, SWEEPS, 8)),
                pltpu.SemaphoreType.DMA((2, SWEEPS, 8)),
            ],
            compiler_params=pltpu.CompilerParams(
                collective_id=0, has_side_effects=True, vmem_limit_bytes=60 * 1024 * 1024
            ),
        )(
            inc.reshape(R * ROWS, U), src.reshape(R * ROWS, U), cls, slot, gain.reshape(64, U), adm, coup, sinv
        )
        half = pl.BlockSpec((R * ROWS // 2, U), lambda i: (i, 0))
        cur, adj = pl.pallas_call(
            last,
            grid=(2,),
            out_shape=(out, out),
            in_specs=[half, half, pl.BlockSpec((ROWS, 2 * T), lambda i: (0, 0)), pl.BlockSpec((U, U), lambda i: (0, 0))],
            out_specs=(half, half),
        )(rest, back, admit, sinv)
        return cur.reshape(R, N, N, U), adj.reshape(R, N, N, U)

    placed = (P(None, "gx", "gy", None), P(None, "gx", "gy", None), P("gx", "gy"), P(), P(), P(), P(), P())
    return jax.shard_map(
        local, mesh=mesh, in_specs=placed, out_specs=(placed[0], placed[0]), check_vma=False
    )
```

```python
import functools

import jax
import jax.numpy as jnp
from jax import lax
from jax.experimental import pallas as pl
from jax.experimental.pallas import tpu as pltpu
from jax.sharding import PartitionSpec as P

MESH = pl.DeviceIdType.MESH
F32 = jnp.float32
BF16 = jnp.bfloat16
SWEEPS = 3
R = 6
N = 16
ROWS = N * N
EDGE = R * N
U = 192
MANY = R * ROWS
T = 128
HALF = 64
STEPS = ((-1, -1), (-1, 0), (-1, 1), (0, -1), (0, 1), (1, -1), (1, 0), (1, 1))
PAIRS = ((0, 5), (1, 6), (2, 7), (3, 4))
TILES = 12
Y_DIRS = ((0, 3, 5), (2, 4, 7))
X_DIRS = ((0, 1, 2), (5, 6, 7))
Y_TILES = ((0, 3, 5, 8, 11), (2, 4, 7, 10, 11))
X_TILES = ((0, 1, 2, 8, 9, 10), (5, 6, 7, 8, 9, 10))


def dot(a, b):
    return jnp.dot(a, b, preferred_element_type=F32)


def dot_nt(a, b):
    return lax.dot_general(a, b, (((1,), (1,)), ((), ())), preferred_element_type=F32)


def iota(shape, dim):
    return lax.broadcasted_iota(jnp.int32, shape, dim)


def low(rows):
    return iota((rows, T), 1) < HALF


def turn(x, shift, axis=0):
    size = x.shape[axis]
    return x if shift % size == 0 else pltpu.roll(x, shift % size, axis)


def spread(tile, corner=None):
    return jnp.concatenate([tile] * R + ([] if corner is None else [corner]), axis=0)


def fold(tile):
    return tile + turn(tile, HALF, 1)


def pack(a, h):
    half = EDGE // 2
    return jnp.concatenate([a, jnp.where(low(half), h[:half], h[half:])], axis=0).astype(BF16)


def unpack(message):
    value = message.astype(F32)
    mixed = value[EDGE:]
    other = turn(mixed, HALF, 1)
    keep = low(EDGE // 2)
    return value[:EDGE], jnp.concatenate([jnp.where(keep, mixed, other), jnp.where(keep, other, mixed)], axis=0)


def kernel(
    nx, ny,
    inc_hbm, src_hbm, cls, slot, gain, adm, coup_hbm, sinv,
    rest_out, back_out, admit_out,
    inc, src, coup, load_sem,
    v0, vm, vp, adj, near_a, near_h, far_a, far_h, gains, lhs, weights, weights_t, partial,
    admit, admit_e, inc_e, src_e, gains_y, gains_x, solve, solve_t, corner_s,
    send_y, send_x, send_c, recv_y, recv_x, recv_c,
    send_sem, recv_sem,
):
    gx, gy = lax.axis_index("gx"), lax.axis_index("gy")
    left, right = lax.rem(gx + nx - 1, nx), lax.rem(gx + 1, nx)
    down, up = lax.rem(gy + ny - 1, ny), lax.rem(gy + 1, ny)
    y_to = ((gx, down), (gx, up))
    x_to = ((left, gy), (right, gy))
    c_to = ((left, down), (right, down), (left, up), (right, up))

    barrier = pltpu.get_barrier_semaphore()
    for where in y_to + x_to + c_to:
        pl.semaphore_signal(barrier, inc=1, device_id=where, device_id_type=MESH)

    loads = [
        pltpu.make_async_copy(a, b, load_sem.at[k])
        for k, (a, b) in enumerate(((inc_hbm, inc), (coup_hbm, coup), (src_hbm, src)))
    ]
    stores = [
        pltpu.make_async_copy(a, b, load_sem.at[3 + k])
        for k, (a, b) in enumerate(((inc, rest_out), (src, back_out), (admit, admit_out)))
    ]
    for load in loads:
        load.start()

    def take(ref):
        parts = [ref[pl.ds(e * (N - 1), EDGE, stride=N), :] for e in range(2)]
        for e in range(2):
            for r in range(R):
                start = r * ROWS + e * (ROWS - N)
                parts.append(ref[start:start + N, :])
        return jnp.concatenate(parts, axis=0)

    def edge_rows(data, a_ref, h_ref, e_ref):
        h_ref[...] = jnp.zeros_like(h_ref)
        for r in range(R):
            a_ref[r * ROWS:(r + 1) * ROWS, :] = data[r * ROWS:(r + 1) * ROWS, 0:T].astype(F32)
            h_ref[r * ROWS:(r + 1) * ROWS, 0:HALF] = data[r * ROWS:(r + 1) * ROWS, T:U].astype(F32)
        for k, ref in enumerate((a_ref, h_ref)):
            columns = slice(k * T, (k + 1) * T)
            e_ref[:, columns] = take(ref)
            ref[...] = jnp.zeros_like(ref)

    def scale_e():
        return jnp.concatenate([spread(admit_e[e * N:(e + 1) * N, :]) for e in range(4)], axis=0)

    def corners(k, value):
        corner_s[k, 0:EDGE, :] = value
        return jnp.concatenate([corner_s[k, pl.ds(0, 8, stride=N), :], corner_s[k, pl.ds(N - 1, 8, stride=N), :]], axis=0)

    def edges_f(v):
        near_e = jnp.concatenate([take(near_a), take(near_h)], axis=1)
        rest = (inc_e[...] - near_e).astype(BF16)
        cur_e = dot(rest[:, 0:U], solve[...]) * scale_e()
        for e in range(2):
            rows = slice(e * EDGE, (e + 1) * EDGE)
            send_y[0, v, e] = pack(cur_e[rows, 0:T], cur_e[rows, T:])
            both = jnp.concatenate([corners(2 * e, cur_e[rows, 0:T]), corners(2 * e + 1, cur_e[rows, T:])], axis=1)
            send_c[0, v, 2 * e] = both[0:8]
            send_c[0, v, 2 * e + 1] = both[8:16]
        for e in range(2):
            rows = slice((2 + e) * EDGE, (3 + e) * EDGE)
            send_x[0, v, e] = pack(cur_e[rows, 0:T], cur_e[rows, T:])

    def edges_a(v):
        far_e = jnp.concatenate([take(far_a), take(far_h)], axis=1)
        back = ((src_e[...] - far_e) * scale_e()).astype(BF16)
        adj_e = dot(back[:, 0:U], solve_t[...])
        for e in range(2):
            rows = slice(e * EDGE, (e + 1) * EDGE)
            cut = [corners(4 + 2 * e + k, adj_e[rows, k * T:(k + 1) * T]) for k in range(2)]
            state = jnp.concatenate([adj_e[rows], jnp.concatenate(cut, axis=1)], axis=0).astype(BF16)
            out = []
            for k, t in enumerate(Y_TILES[e]):
                gain_k = gains_y[e, :, k * T:(k + 1) * T]
                out.append(dot(state, weights_t[:, t * T:(t + 1) * T]) * spread(gain_k[0:N], gain_k[N:]))
            part_a = turn(out[0][:EDGE], -1) + out[1][:EDGE] + turn(out[2][:EDGE], 1)
            part_h = fold(
                jnp.where(low(EDGE), turn(out[3][:EDGE], -1), turn(out[3][:EDGE], 1)) + out[4][:EDGE]
            )
            tail_a = out[0][EDGE:] + out[1][EDGE:] + out[2][EDGE:]
            tail_h = fold(out[3][EDGE:] + out[4][EDGE:])
            send_y[1, v, e] = pack(part_a, part_h)
            tail = jnp.concatenate([tail_a, tail_h], axis=1)
            send_c[1, v, 2 * e] = tail[0:8]
            send_c[1, v, 2 * e + 1] = tail[8:16]
        for e in range(2):
            state = adj_e[(2 + e) * EDGE:(3 + e) * EDGE].astype(BF16)
            out = []
            for k, t in enumerate(X_TILES[e]):
                out.append(dot(state, weights_t[:, t * T:(t + 1) * T]) * spread(gains_x[e, :, k * T:(k + 1) * T]))
            part_a = turn(out[0], -1) + out[1] + turn(out[2], 1)
            part_h = fold(turn(out[3], -1) + out[4] + turn(out[5], 1))
            send_x[1, v, e] = pack(part_a, part_h)

    inside_y = (gy > 0, gy < ny - 1)
    inside_x = (gx > 0, gx < nx - 1)

    def copies(kind, v):
        made = []
        for e in range(2):
            made.append((send_y.at[kind, v, e], recv_y.at[kind, v, 1 - e], y_to[e], e, 1 - e, inside_y[e], inside_y[1 - e]))
        for e in range(2):
            made.append((send_x.at[kind, v, e], recv_x.at[kind, v, 1 - e], x_to[e], 2 + e, 3 - e, inside_x[e], inside_x[1 - e]))
        for q in range(4):
            goes = inside_y[q // 2] & inside_x[q % 2]
            comes = inside_y[1 - q // 2] & inside_x[1 - q % 2]
            made.append((send_c.at[kind, v, q], recv_c.at[kind, v, 3 - q], c_to[q], 4 + q, 7 - q, goes, comes))
        return [
            (
                pltpu.make_async_remote_copy(
                    src_ref=a, dst_ref=b, send_sem=send_sem.at[kind, v, s], recv_sem=recv_sem.at[kind, v, t],
                    device_id=where, device_id_type=MESH,
                ),
                goes,
                comes,
            )
            for a, b, where, s, t, goes, comes in made
        ]

    def start(kind, v):
        for copy, goes, _ in copies(kind, v):
            pl.when(goes)(copy.start)

    def arrive(kind, v):
        for copy, _, comes in copies(kind, v):
            pl.when(comes)(copy.wait_recv)

    def sent(kind, v):
        for copy, goes, _ in copies(kind, v):
            pl.when(goes)(copy.wait_send)

    def no_sender():
        def clear(ref, q):
            for kind in range(2):
                for v in range(SWEEPS):
                    ref[kind, v, q] = jnp.zeros(ref.shape[3:], ref.dtype)

        for e in range(2):
            pl.when(jnp.logical_not(inside_y[e]))(functools.partial(clear, recv_y, e))
            pl.when(jnp.logical_not(inside_x[e]))(functools.partial(clear, recv_x, e))
        for q in range(4):
            pl.when(jnp.logical_not(inside_y[q // 2] & inside_x[q % 2]))(functools.partial(clear, recv_c, q))

    def right_f():
        near = jnp.concatenate([near_a[0:MANY, :], near_h[0:MANY, 0:HALF]], axis=1)
        return (inc[...].astype(F32) - near).astype(BF16)

    def right_a():
        far = jnp.concatenate([far_a[0:MANY, :], far_h[0:MANY, 0:HALF]], axis=1)
        back = src[...].astype(F32) - far
        back = [back[r * ROWS:(r + 1) * ROWS] * admit[:, 0:U] for r in range(R)]
        return jnp.concatenate(back, axis=0).astype(BF16)

    shifted = {-1: vm, 0: v0, 1: vp}

    def main_f():
        cur = dot(right_f(), solve[...])
        for r in range(R):
            one_cur = cur[r * ROWS:(r + 1) * ROWS] * admit[...]
            v0[r, N:N + ROWS, :] = one_cur.astype(BF16)
            vm[r, N:N + ROWS, :] = turn(one_cur, 1).astype(BF16)
            vp[r, N:N + ROWS, :] = turn(one_cur, -1).astype(BF16)
        for r in range(R):
            rows = slice(r * ROWS, (r + 1) * ROWS)

            def nearby(d, columns):
                sx, sy = STEPS[d]
                return shifted[sy][r, N * (1 + sx):N * (1 + sx) + ROWS, columns]

            for d in range(8):
                columns = slice(d * T, (d + 1) * T)
                lhs[rows, columns] = nearby(d, slice(0, T)) * gains[:, columns]
            for p, (d0, d1) in enumerate(PAIRS):
                columns = slice((8 + p) * T, (9 + p) * T)
                both = jnp.where(low(ROWS), nearby(d0, slice(T, 2 * T)), nearby(d1, slice(T, 2 * T)))
                lhs[rows, columns] = both * gains[:, columns]
        near = dot(lhs[...], weights[...])
        near_a[0:MANY, :] = near[:, 0:T]
        near_h[0:MANY, :] = near[:, T:]

    def main_a():
        adj[...] = dot(right_a(), solve_t[...]).astype(BF16)
        for t in range(TILES // 2):
            columns = slice(2 * t * T, 2 * (t + 1) * T)
            value = dot(adj[...], weights_t[:, columns]).astype(BF16)
            for r in range(R):
                partial[r, N:N + ROWS, columns] = value[r * ROWS:(r + 1) * ROWS] * gains[:, columns]
        for r in range(R):

            def part(x, t):
                return partial[r, x * N:(x + 1) * N, t * T:(t + 1) * T].astype(F32)

            for x in range(N):
                sums = {sy: None for sy in (-1, 0, 1)}
                for d, (sx, sy) in enumerate(STEPS):
                    value = part(1 + x - sx, d)
                    sums[sy] = value if sums[sy] is None else sums[sy] + value
                a = turn(sums[1], 1) + sums[0] + turn(sums[-1], -1)
                tops = {sy: jnp.where(low(N), part(2 + x, 9 + sy), part(x, 9 + sy)) for sy in (-1, 0, 1)}
                mid = part(1 + x, 11)
                below = tops[-1] + jnp.where(low(N), mid, 0.0)
                above = tops[1] + jnp.where(low(N), 0.0, mid)
                h = fold(turn(above, 1) + tops[0] + turn(below, -1))
                at = r * ROWS + x * N
                far_a[at:at + N, :] = a
                far_h[at:at + N, :] = h

    def add_y(e, ref, value, tail):
        y0 = e * (N - 1)
        for at, piece in (
            (pl.ds(y0, EDGE, stride=N), value),
            (pl.ds(y0, 8, stride=ROWS), tail[0:8]),
            (pl.ds(y0 + ROWS - N, 8, stride=ROWS), tail[8:16]),
        ):
            ref[at, :] = ref[at, :] + piece

    def add_x(e, ref, value):
        for r in range(R):
            at = r * ROWS + e * (ROWS - N)
            ref[at:at + N, :] = ref[at:at + N, :] + value[r * N:(r + 1) * N]

    def correct_f(v):
        for e in range(2):
            a, h = unpack(recv_y[0, v, e])
            tail = jnp.concatenate([recv_c[0, v, 2 * e], recv_c[0, v, 2 * e + 1]], axis=0)
            tail_a, tail_h = tail[:, 0:T], tail[:, T:]
            tiles = [
                (turn(a, 1), tail_a), (a, tail_a), (turn(a, -1), tail_a),
                (jnp.where(low(EDGE), turn(h, 1), turn(h, -1)), tail_h), (h, tail_h),
            ]
            scaled = []
            for k, tile in enumerate(tiles):
                gain_k = gains_y[e, :, k * T:(k + 1) * T]
                scaled.append((jnp.concatenate(tile, axis=0) * spread(gain_k[0:N], gain_k[N:])).astype(BF16))
            matrix = jnp.concatenate([weights[t * T:(t + 1) * T, :] for t in Y_TILES[e]], axis=0)
            extra = dot(jnp.concatenate(scaled, axis=1), matrix)
            add_y(e, near_a, extra[:EDGE, 0:T], extra[EDGE:, 0:T])
            add_y(e, near_h, extra[:EDGE, T:], extra[EDGE:, T:])
        for e in range(2):
            a, h = unpack(recv_x[0, v, e])
            tiles = [turn(a, 1), a, turn(a, -1), turn(h, 1), h, turn(h, -1)]
            scaled = []
            for k, tile in enumerate(tiles):
                scaled.append((tile * spread(gains_x[e, :, k * T:(k + 1) * T])).astype(BF16))
            matrix = jnp.concatenate([weights[t * T:(t + 1) * T, :] for t in X_TILES[e]], axis=0)
            extra = dot(jnp.concatenate(scaled, axis=1), matrix)
            add_x(e, near_a, extra[:, 0:T])
            add_x(e, near_h, extra[:, T:])

    def correct_a(v):
        for e in range(2):
            a, h = unpack(recv_y[1, v, e])
            tail = jnp.concatenate([recv_c[1, v, 2 * e], recv_c[1, v, 2 * e + 1]], axis=0)
            add_y(e, far_a, a, tail[:, 0:T])
            add_y(e, far_h, h, tail[:, T:])
        for e in range(2):
            a, h = unpack(recv_x[1, v, e])
            add_x(e, far_a, a)
            add_x(e, far_h, h)

    one = jnp.float32(1.0)
    has_left, has_right = jnp.where(gx > 0, 1.0, 0.0) * one, jnp.where(gx < nx - 1, 1.0, 0.0) * one
    has_down, has_up = jnp.where(gy > 0, 1.0, 0.0) * one, jnp.where(gy < ny - 1, 1.0, 0.0) * one

    def chooser(rows, columns, wanted):
        return jnp.where(iota((rows, columns), 0) == wanted, 1.0, 0.0).astype(BF16)

    lane = iota((U, 2 * T), 1)
    dup = chooser(U, 2 * T, jnp.where(lane < U, lane, lane - HALF))
    dup_back = chooser(U, 2 * T, jnp.where(lane < HALF, lane + T, jnp.where(lane < T, lane + HALF, lane - T)))
    eye = chooser(U, U, iota((U, U), 1))
    solve[...] = dot(sinv[...], dup).astype(BF16)
    solve_n = dot_nt(eye, sinv[...]).astype(BF16)
    solve_t[...] = dot(solve_n, dup_back).astype(BF16)

    adm_high = adm[...].astype(BF16).astype(F32)
    adm_both = jnp.concatenate([adm_high, adm[...] - adm_high], axis=0).astype(BF16)
    adm_table = dot(adm_both, dup).astype(BF16)

    diag = iota((N, N), 0) == iota((N, N), 1)
    spots = [jnp.where(diag, cls[x:x + 1, :].astype(F32), 0.0) for x in range(N)]
    kind = dot(jnp.concatenate(spots, axis=0).astype(BF16), jnp.ones((N, N), BF16))

    def onehot(kinds):
        which = lax.rem(iota((kinds.shape[0], N), 1), 8)
        return jnp.where(which.astype(F32) == kinds, 1.0, 0.0).astype(BF16)

    kind_e = jnp.concatenate(
        [
            jnp.broadcast_to(cls[:, 0:1].astype(F32), (N, N)),
            jnp.broadcast_to(cls[:, N - 1:N].astype(F32), (N, N)),
            kind[0:N],
            kind[ROWS - N:ROWS],
        ],
        axis=0,
    )
    hot, hot_e = onehot(kind), onehot(kind_e)
    admit_e[...] = dot(hot_e, adm_table)
    corner_s[...] = jnp.zeros_like(corner_s)
    no_sender()
    loads[0].wait()
    edge_rows(inc, near_a, near_h, inc_e)
    pick = [
        jnp.where(iota((8, 64), 1) == iota((8, 64), 0) * 8 + slot[:, d:d + 1], 1.0, 0.0)
        for d in range(8)
    ]
    pick = jnp.concatenate(pick, axis=0).astype(BF16)
    gain_dup = dot(gain[...].astype(BF16), dup).astype(BF16)
    table64 = dot(pick, gain_dup)
    pieces = [table64[d * 8:(d + 1) * 8, 0:T] for d in range(8)]
    for d0, d1 in PAIRS:
        pieces.append(jnp.where(low(8), table64[d0 * 8:(d0 + 1) * 8, T:], table64[d1 * 8:(d1 + 1) * 8, T:]))
    table = jnp.concatenate(pieces, axis=1)
    table = jnp.concatenate([table, jnp.zeros_like(table)], axis=0).astype(BF16)
    edge_gain = dot(hot_e, table)
    spot = iota((N, T), 0)

    def along(j):
        return jnp.where((spot + j >= 0) & (spot + j < N), 1.0, 0.0)

    lows = jnp.where(low(N), 1.0, 0.0)
    for e, exists in enumerate((has_down, has_up)):
        raw = edge_gain[e * N:(e + 1) * N]
        first = jnp.where(spot < 8, 1.0, 0.0)
        side = first * has_left + (1.0 - first) * has_right
        for k, t in enumerate(Y_TILES[e]):
            tile = raw[:, t * T:(t + 1) * T]
            ends = jnp.where(spot < 8, jnp.broadcast_to(tile[0:1], (N, T)), jnp.broadcast_to(tile[N - 1:N], (N, T)))
            if k < 3:
                keep = along(k - 1)
                corner = (first, 0.0 * first, 1.0 - first)[k]
            elif k == 3:
                keep = lows * along(-1) + (1.0 - lows) * along(1)
                corner = lows * first + (1.0 - lows) * (1.0 - first)
            else:
                keep = lows if e == 0 else 1.0 - lows
                corner = 0.0 * first
            gains_y[e, 0:N, k * T:(k + 1) * T] = tile * keep * exists
            gains_y[e, N:2 * N, k * T:(k + 1) * T] = ends * corner * side * exists
    for e, exists in enumerate((has_left, has_right)):
        raw = edge_gain[(2 + e) * N:(3 + e) * N]
        for k, t in enumerate(X_TILES[e]):
            keep = along(k % 3 - 1)
            if k >= 3:
                keep = keep * (lows if e == 0 else 1.0 - lows)
            gains_x[e, :, k * T:(k + 1) * T] = raw[:, t * T:(t + 1) * T] * keep * exists

    loads[1].wait()
    weights[...] = jnp.zeros_like(weights)
    for d in range(8):
        weights[d * T:(d + 1) * T, 0:U] = coup[d, 0:T, :]
    for p, (d0, d1) in enumerate(PAIRS):
        base = (8 + p) * T
        weights[base:base + HALF, 0:U] = coup[d0, T:U, :]
        weights[base + HALF:base + T, 0:U] = coup[d1, T:U, :]
    row = iota((2 * T, U), 0)
    place = jnp.where(row < HALF, -1, jnp.where(row < T, row + HALF, row - T))
    order = jnp.where(iota((2 * T, U), 1) == place, 1.0, 0.0).astype(BF16)
    for t in range(TILES):
        weights_t[:, t * T:(t + 1) * T] = dot_nt(order, weights[t * T:(t + 1) * T, 0:U]).astype(BF16)

    loads[2].wait()
    edge_rows(src, far_a, far_h, src_e)

    admit[...] = dot(hot, adm_table)
    stores[2].start()

    def inside(rows, sx, sy):
        r = iota((rows, T), 0)
        x, y = r // N + sx, lax.rem(r, N) + sy
        return (x >= 0) & (x < N) & (y >= 0) & (y < N)

    for t in range(TILES):
        value = dot(hot, table[:, t * T:(t + 1) * T])
        if t < 8:
            keep = jnp.where(inside(ROWS, *STEPS[t]), 1.0, 0.0)
        else:
            d0, d1 = PAIRS[t - 8]
            keep = jnp.where(
                low(ROWS), jnp.where(inside(ROWS, *STEPS[d0]), 1.0, 0.0), jnp.where(inside(ROWS, *STEPS[d1]), 1.0, 0.0)
            )
        gains[:, t * T:(t + 1) * T] = (value * keep).astype(BF16)

    for ref in (v0, vm, vp):
        for r in range(R):
            ref[r, 0:N, :] = jnp.zeros((N, 2 * T), BF16)
            ref[r, (N + 1) * N:(N + 2) * N, :] = jnp.zeros((N, 2 * T), BF16)
    for r in range(R):
        partial[r, 0:N, :] = jnp.zeros((N, TILES * T), BF16)
        partial[r, (N + 1) * N:(N + 2) * N, :] = jnp.zeros((N, TILES * T), BF16)

    edges_f(0)
    edges_a(0)
    pl.semaphore_wait(barrier, 8)
    start(0, 0)
    start(1, 0)
    main_f()

    def sweep(v, carry):
        main_a()
        arrive(0, v)
        correct_f(v)
        edges_f(v + 1)
        start(0, v + 1)
        main_f()
        arrive(1, v)
        correct_a(v)
        edges_a(v + 1)
        start(1, v + 1)
        return carry

    for v in range(SWEEPS - 1):
        sweep(v, 0)
    main_a()
    arrive(0, SWEEPS - 1)
    correct_f(SWEEPS - 1)
    inc[...] = right_f()
    stores[0].start()
    arrive(1, SWEEPS - 1)
    correct_a(SWEEPS - 1)
    src[...] = right_a()
    stores[1].start()
    for kind in range(2):
        for v in range(SWEEPS):
            sent(kind, v)
    for store in stores:
        store.wait()


def last(rest, back, admit, sinv, cur_out, adj_out):
    cur = dot(rest[...], sinv[...])
    for r in range(R // 2):
        rows = slice(r * ROWS, (r + 1) * ROWS)
        cur_out[rows, :] = (cur[rows] * admit[:, 0:U]).astype(BF16)
    adj_out[...] = dot_nt(back[...], sinv[...]).astype(BF16)


def solution(mesh):
    nx, ny = mesh.shape["gx"], mesh.shape["gy"]

    def local(inc, src, cls, slot, gain, adm, coup, sinv):
        vmem = pl.BlockSpec(memory_space=pltpu.VMEM)
        anywhere = pl.BlockSpec(memory_space=pl.ANY)
        out = jax.ShapeDtypeStruct((R * ROWS, U), BF16)
        rest, back, admit = pl.pallas_call(
            functools.partial(kernel, nx, ny),
            out_shape=(out, out, jax.ShapeDtypeStruct((ROWS, 2 * T), F32)),
            in_specs=[anywhere, anywhere, vmem, vmem, vmem, vmem, anywhere, vmem],
            out_specs=(anywhere, anywhere, anywhere),
            scratch_shapes=[
                pltpu.VMEM((R * ROWS, U), BF16),
                pltpu.VMEM((R * ROWS, U), BF16),
                pltpu.VMEM((8, U, U), BF16),
                pltpu.SemaphoreType.DMA((6,)),
                pltpu.VMEM((R, ROWS + 2 * N, 2 * T), BF16),
                pltpu.VMEM((R, ROWS + 2 * N, 2 * T), BF16),
                pltpu.VMEM((R, ROWS + 2 * N, 2 * T), BF16),
                pltpu.VMEM((R * ROWS, 2 * T), BF16),
                pltpu.VMEM((8 * ROWS, T), F32),
                pltpu.VMEM((8 * ROWS, T), F32),
                pltpu.VMEM((8 * ROWS, T), F32),
                pltpu.VMEM((8 * ROWS, T), F32),
                pltpu.VMEM((ROWS, TILES * T), BF16),
                pltpu.VMEM((R * ROWS, TILES * T), BF16),
                pltpu.VMEM((TILES * T, 2 * T), BF16),
                pltpu.VMEM((2 * T, TILES * T), BF16),
                pltpu.VMEM((R, ROWS + 2 * N, TILES * T), BF16),
                pltpu.VMEM((ROWS, 2 * T), F32),
                pltpu.VMEM((4 * N, 2 * T), F32),
                pltpu.VMEM((4 * EDGE, 2 * T), F32),
                pltpu.VMEM((4 * EDGE, 2 * T), F32),
                pltpu.VMEM((2, 2 * N, 5 * T), F32),
                pltpu.VMEM((2, N, 6 * T), F32),
                pltpu.VMEM((U, 2 * T), BF16),
                pltpu.VMEM((U, 2 * T), BF16),
                pltpu.VMEM((8, 8 * N, T), F32),
                pltpu.VMEM((2, SWEEPS, 2, EDGE + EDGE // 2, T), BF16),
                pltpu.VMEM((2, SWEEPS, 2, EDGE + EDGE // 2, T), BF16),
                pltpu.VMEM((2, SWEEPS, 4, 8, 2 * T), F32),
                pltpu.VMEM((2, SWEEPS, 2, EDGE + EDGE // 2, T), BF16),
                pltpu.VMEM((2, SWEEPS, 2, EDGE + EDGE // 2, T), BF16),
                pltpu.VMEM((2, SWEEPS, 4, 8, 2 * T), F32),
                pltpu.SemaphoreType.DMA((2, SWEEPS, 8)),
                pltpu.SemaphoreType.DMA((2, SWEEPS, 8)),
            ],
            compiler_params=pltpu.CompilerParams(
                collective_id=0, has_side_effects=True, vmem_limit_bytes=60 * 1024 * 1024
            ),
        )(
            inc.reshape(R * ROWS, U), src.reshape(R * ROWS, U), cls, slot, gain.reshape(64, U), adm, coup, sinv
        )
        half = pl.BlockSpec((R * ROWS // 2, U), lambda i: (i, 0))
        cur, adj = pl.pallas_call(
            last,
            grid=(2,),
            out_shape=(out, out),
            in_specs=[half, half, pl.BlockSpec((ROWS, 2 * T), lambda i: (0, 0)), pl.BlockSpec((U, U), lambda i: (0, 0))],
            out_specs=(half, half),
        )(rest, back, admit, sinv)
        return cur.reshape(R, N, N, U), adj.reshape(R, N, N, U)

    placed = (P(None, "gx", "gy", None), P(None, "gx", "gy", None), P("gx", "gy"), P(), P(), P(), P(), P())
    return jax.shard_map(
        local, mesh=mesh, in_specs=placed, out_specs=(placed[0], placed[0]), check_vma=False
    )
```

```python
import functools

import jax
import jax.numpy as jnp
from jax import lax
from jax.experimental import pallas as pl
from jax.experimental.pallas import tpu as pltpu
from jax.sharding import PartitionSpec as P

MESH = pl.DeviceIdType.MESH
F32 = jnp.float32
BF16 = jnp.bfloat16
SWEEPS = 3
R = 6
N = 16
ROWS = N * N
EDGE = R * N
U = 192
MANY = R * ROWS
T = 128
HALF = 64
STEPS = ((-1, -1), (-1, 0), (-1, 1), (0, -1), (0, 1), (1, -1), (1, 0), (1, 1))
PAIRS = ((0, 5), (1, 6), (2, 7), (3, 4))
TILES = 12
Y_DIRS = ((0, 3, 5), (2, 4, 7))
X_DIRS = ((0, 1, 2), (5, 6, 7))
Y_TILES = ((0, 3, 5, 8, 11), (2, 4, 7, 10, 11))
X_TILES = ((0, 1, 2, 8, 9, 10), (5, 6, 7, 8, 9, 10))


def dot(a, b):
    return jnp.dot(a, b, preferred_element_type=F32)


def dot_nt(a, b):
    return lax.dot_general(a, b, (((1,), (1,)), ((), ())), preferred_element_type=F32)


def iota(shape, dim):
    return lax.broadcasted_iota(jnp.int32, shape, dim)


def low(rows):
    return iota((rows, T), 1) < HALF


def turn(x, shift, axis=0):
    size = x.shape[axis]
    return x if shift % size == 0 else pltpu.roll(x, shift % size, axis)


def spread(tile, corner=None):
    return jnp.concatenate([tile] * R + ([] if corner is None else [corner]), axis=0)


def fold(tile):
    return tile + turn(tile, HALF, 1)


def pack(a, h):
    half = EDGE // 2
    return jnp.concatenate([a, jnp.where(low(half), h[:half], h[half:])], axis=0).astype(BF16)


def unpack(message):
    value = message.astype(F32)
    mixed = value[EDGE:]
    other = turn(mixed, HALF, 1)
    keep = low(EDGE // 2)
    return value[:EDGE], jnp.concatenate([jnp.where(keep, mixed, other), jnp.where(keep, other, mixed)], axis=0)


def kernel(
    nx, ny,
    inc_hbm, src_hbm, cls, slot, gain, adm, coup_hbm, sinv,
    rest_out, back_out, admit_out,
    inc, src, coup, load_sem, gains_w,
    v0, vm, vp, adj, near_a, near_h, far_a, far_h, gains, lhs, weights, weights_t, partial,
    admit, admit_e, inc_e, src_e, gains_y, gains_x, solve, solve_t, corner_s,
    send_y, send_x, send_c, recv_y, recv_x, recv_c,
    send_sem, recv_sem,
):
    gx, gy = lax.axis_index("gx"), lax.axis_index("gy")
    left, right = lax.rem(gx + nx - 1, nx), lax.rem(gx + 1, nx)
    down, up = lax.rem(gy + ny - 1, ny), lax.rem(gy + 1, ny)
    y_to = ((gx, down), (gx, up))
    x_to = ((left, gy), (right, gy))
    c_to = ((left, down), (right, down), (left, up), (right, up))

    barrier = pltpu.get_barrier_semaphore()
    for where in y_to + x_to + c_to:
        pl.semaphore_signal(barrier, inc=1, device_id=where, device_id_type=MESH)

    loads = [
        pltpu.make_async_copy(a, b, load_sem.at[k])
        for k, (a, b) in enumerate(((inc_hbm, inc), (coup_hbm, coup), (src_hbm, src)))
    ]
    stores = [
        pltpu.make_async_copy(a, b, load_sem.at[3 + k])
        for k, (a, b) in enumerate(((inc, rest_out), (src, back_out), (admit, admit_out)))
    ]
    for load in loads:
        load.start()

    def take(ref):
        parts = [ref[pl.ds(e * (N - 1), EDGE, stride=N), :] for e in range(2)]
        for e in range(2):
            for r in range(R):
                start = r * ROWS + e * (ROWS - N)
                parts.append(ref[start:start + N, :])
        return jnp.concatenate(parts, axis=0)

    def edge_rows(data, a_ref, h_ref, e_ref):
        h_ref[...] = jnp.zeros_like(h_ref)
        for r in range(R):
            a_ref[r * ROWS:(r + 1) * ROWS, :] = data[r * ROWS:(r + 1) * ROWS, 0:T].astype(F32)
            h_ref[r * ROWS:(r + 1) * ROWS, 0:HALF] = data[r * ROWS:(r + 1) * ROWS, T:U].astype(F32)
        for k, ref in enumerate((a_ref, h_ref)):
            columns = slice(k * T, (k + 1) * T)
            e_ref[:, columns] = take(ref)
            ref[...] = jnp.zeros_like(ref)

    def scale_e():
        return jnp.concatenate([spread(admit_e[e * N:(e + 1) * N, :]) for e in range(4)], axis=0)

    def corners(k, value):
        corner_s[k, 0:EDGE, :] = value
        return jnp.concatenate([corner_s[k, pl.ds(0, 8, stride=N), :], corner_s[k, pl.ds(N - 1, 8, stride=N), :]], axis=0)

    def edges_f(v):
        near_e = jnp.concatenate([take(near_a), take(near_h)], axis=1)
        rest = (inc_e[...] - near_e).astype(BF16)
        cur_e = dot(rest[:, 0:U], solve[...]) * scale_e()
        for e in range(2):
            rows = slice(e * EDGE, (e + 1) * EDGE)
            send_y[0, v, e] = pack(cur_e[rows, 0:T], cur_e[rows, T:])
            both = jnp.concatenate([corners(2 * e, cur_e[rows, 0:T]), corners(2 * e + 1, cur_e[rows, T:])], axis=1)
            send_c[0, v, 2 * e] = both[0:8]
            send_c[0, v, 2 * e + 1] = both[8:16]
        for e in range(2):
            rows = slice((2 + e) * EDGE, (3 + e) * EDGE)
            send_x[0, v, e] = pack(cur_e[rows, 0:T], cur_e[rows, T:])

    def products(state, tiles):
        out = []
        for k in range(0, len(tiles), 2):
            two = tiles[k:k + 2]
            value = dot(state, jnp.concatenate([weights_t[:, t * T:(t + 1) * T] for t in two], axis=1))
            out += [value[:, i * T:(i + 1) * T] for i in range(len(two))]
        return out

    def edges_a(v):
        far_e = jnp.concatenate([take(far_a), take(far_h)], axis=1)
        back = ((src_e[...] - far_e) * scale_e()).astype(BF16)
        adj_e = dot(back[:, 0:U], solve_t[...])
        for e in range(2):
            rows = slice(e * EDGE, (e + 1) * EDGE)
            cut = [corners(4 + 2 * e + k, adj_e[rows, k * T:(k + 1) * T]) for k in range(2)]
            state = jnp.concatenate([adj_e[rows], jnp.concatenate(cut, axis=1)], axis=0).astype(BF16)
            out = []
            for k, value in enumerate(products(state, Y_TILES[e])):
                gain_k = gains_y[e, :, k * T:(k + 1) * T]
                out.append(value * spread(gain_k[0:N], gain_k[N:]))
            part_a = turn(out[0][:EDGE], -1) + out[1][:EDGE] + turn(out[2][:EDGE], 1)
            part_h = fold(
                jnp.where(low(EDGE), turn(out[3][:EDGE], -1), turn(out[3][:EDGE], 1)) + out[4][:EDGE]
            )
            tail_a = out[0][EDGE:] + out[1][EDGE:] + out[2][EDGE:]
            tail_h = fold(out[3][EDGE:] + out[4][EDGE:])
            send_y[1, v, e] = pack(part_a, part_h)
            tail = jnp.concatenate([tail_a, tail_h], axis=1)
            send_c[1, v, 2 * e] = tail[0:8]
            send_c[1, v, 2 * e + 1] = tail[8:16]
        for e in range(2):
            state = adj_e[(2 + e) * EDGE:(3 + e) * EDGE].astype(BF16)
            out = []
            for k, value in enumerate(products(state, X_TILES[e])):
                out.append(value * spread(gains_x[e, :, k * T:(k + 1) * T]))
            part_a = turn(out[0], -1) + out[1] + turn(out[2], 1)
            part_h = fold(turn(out[3], -1) + out[4] + turn(out[5], 1))
            send_x[1, v, e] = pack(part_a, part_h)

    inside_y = (gy > 0, gy < ny - 1)
    inside_x = (gx > 0, gx < nx - 1)

    def copies(kind, v):
        made = []
        for e in range(2):
            made.append((send_y.at[kind, v, e], recv_y.at[kind, v, 1 - e], y_to[e], e, 1 - e, inside_y[e], inside_y[1 - e]))
        for e in range(2):
            made.append((send_x.at[kind, v, e], recv_x.at[kind, v, 1 - e], x_to[e], 2 + e, 3 - e, inside_x[e], inside_x[1 - e]))
        for q in range(4):
            goes = inside_y[q // 2] & inside_x[q % 2]
            comes = inside_y[1 - q // 2] & inside_x[1 - q % 2]
            made.append((send_c.at[kind, v, q], recv_c.at[kind, v, 3 - q], c_to[q], 4 + q, 7 - q, goes, comes))
        return [
            (
                pltpu.make_async_remote_copy(
                    src_ref=a, dst_ref=b, send_sem=send_sem.at[kind, v, s], recv_sem=recv_sem.at[kind, v, t],
                    device_id=where, device_id_type=MESH,
                ),
                goes,
                comes,
            )
            for a, b, where, s, t, goes, comes in made
        ]

    def start(kind, v):
        for copy, goes, _ in copies(kind, v):
            pl.when(goes)(copy.start)

    def arrive(kind, v):
        for copy, _, comes in copies(kind, v):
            pl.when(comes)(copy.wait_recv)

    def sent(kind, v):
        for copy, goes, _ in copies(kind, v):
            pl.when(goes)(copy.wait_send)

    def no_sender():
        def clear(ref, q):
            for kind in range(2):
                for v in range(SWEEPS):
                    ref[kind, v, q] = jnp.zeros(ref.shape[3:], ref.dtype)

        for e in range(2):
            pl.when(jnp.logical_not(inside_y[e]))(functools.partial(clear, recv_y, e))
            pl.when(jnp.logical_not(inside_x[e]))(functools.partial(clear, recv_x, e))
        for q in range(4):
            pl.when(jnp.logical_not(inside_y[q // 2] & inside_x[q % 2]))(functools.partial(clear, recv_c, q))

    def right_f():
        near = jnp.concatenate([near_a[0:MANY, :], near_h[0:MANY, 0:HALF]], axis=1)
        return (inc[...].astype(F32) - near).astype(BF16)

    def right_a():
        far = jnp.concatenate([far_a[0:MANY, :], far_h[0:MANY, 0:HALF]], axis=1)
        back = src[...].astype(F32) - far
        back = [back[r * ROWS:(r + 1) * ROWS] * admit[:, 0:U] for r in range(R)]
        return jnp.concatenate(back, axis=0).astype(BF16)

    shifted = {-1: vm, 0: v0, 1: vp}

    halves = (slice(0, MANY // 2), slice(MANY // 2, MANY))

    def main_f():
        rest = right_f()
        cur = jnp.concatenate([dot(rest[rows], solve[...]) for rows in halves], axis=0)
        for r in range(R):
            one_cur = cur[r * ROWS:(r + 1) * ROWS] * admit[...]
            v0[r, N:N + ROWS, :] = one_cur.astype(BF16)
            vm[r, N:N + ROWS, :] = turn(one_cur, 1).astype(BF16)
            vp[r, N:N + ROWS, :] = turn(one_cur, -1).astype(BF16)
        for r in range(R):
            rows = slice(r * ROWS, (r + 1) * ROWS)

            def nearby(d, columns):
                sx, sy = STEPS[d]
                return shifted[sy][r, N * (1 + sx):N * (1 + sx) + ROWS, columns]

            for d in range(8):
                columns = slice(d * T, (d + 1) * T)
                lhs[rows, columns] = nearby(d, slice(0, T)) * gains[:, columns]
            for p, (d0, d1) in enumerate(PAIRS):
                columns = slice((8 + p) * T, (9 + p) * T)
                both = jnp.where(low(ROWS), nearby(d0, slice(T, 2 * T)), nearby(d1, slice(T, 2 * T)))
                lhs[rows, columns] = both * gains[:, columns]
        for rows in halves:
            near = dot(lhs[rows, :], weights[...])
            near_a[rows, :] = near[:, 0:T]
            near_h[rows, :] = near[:, T:]

    def main_a():
        back = right_a()
        for rows in halves:
            adj[rows, :] = dot(back[rows], solve_t[...]).astype(BF16)
        for t in range(TILES // 2):
            columns = slice(2 * t * T, 2 * (t + 1) * T)
            value = dot(adj[...], weights_t[:, columns])
            for r in range(R):
                partial[r, N:N + ROWS, columns] = value[r * ROWS:(r + 1) * ROWS] * gains_w[:, columns]
        for r in range(R):

            def part(x, t):
                return partial[r, x * N:(x + 1) * N, t * T:(t + 1) * T]

            for x in range(N):
                sums = {sy: None for sy in (-1, 0, 1)}
                for d, (sx, sy) in enumerate(STEPS):
                    value = part(1 + x - sx, d)
                    sums[sy] = value if sums[sy] is None else sums[sy] + value
                a = turn(sums[1], 1) + sums[0] + turn(sums[-1], -1)
                tops = {sy: jnp.where(low(N), part(2 + x, 9 + sy), part(x, 9 + sy)) for sy in (-1, 0, 1)}
                mid = part(1 + x, 11)
                below = tops[-1] + jnp.where(low(N), mid, 0.0)
                above = tops[1] + jnp.where(low(N), 0.0, mid)
                h = fold(turn(above, 1) + tops[0] + turn(below, -1))
                at = r * ROWS + x * N
                far_a[at:at + N, :] = a
                far_h[at:at + N, :] = h

    def add_y(e, ref, value, tail):
        y0 = e * (N - 1)
        for at, piece in (
            (pl.ds(y0, EDGE, stride=N), value),
            (pl.ds(y0, 8, stride=ROWS), tail[0:8]),
            (pl.ds(y0 + ROWS - N, 8, stride=ROWS), tail[8:16]),
        ):
            ref[at, :] = ref[at, :] + piece

    def add_x(e, ref, value):
        for r in range(R):
            at = r * ROWS + e * (ROWS - N)
            ref[at:at + N, :] = ref[at:at + N, :] + value[r * N:(r + 1) * N]

    def correct_f(v):
        for e in range(2):
            a, h = unpack(recv_y[0, v, e])
            tail = jnp.concatenate([recv_c[0, v, 2 * e], recv_c[0, v, 2 * e + 1]], axis=0)
            tail_a, tail_h = tail[:, 0:T], tail[:, T:]
            tiles = [
                (turn(a, 1), tail_a), (a, tail_a), (turn(a, -1), tail_a),
                (jnp.where(low(EDGE), turn(h, 1), turn(h, -1)), tail_h), (h, tail_h),
            ]
            scaled = []
            for k, tile in enumerate(tiles):
                gain_k = gains_y[e, :, k * T:(k + 1) * T]
                scaled.append((jnp.concatenate(tile, axis=0) * spread(gain_k[0:N], gain_k[N:])).astype(BF16))
            matrix = jnp.concatenate([weights[t * T:(t + 1) * T, :] for t in Y_TILES[e]], axis=0)
            extra = dot(jnp.concatenate(scaled, axis=1), matrix)
            add_y(e, near_a, extra[:EDGE, 0:T], extra[EDGE:, 0:T])
            add_y(e, near_h, extra[:EDGE, T:], extra[EDGE:, T:])
        for e in range(2):
            a, h = unpack(recv_x[0, v, e])
            tiles = [turn(a, 1), a, turn(a, -1), turn(h, 1), h, turn(h, -1)]
            scaled = []
            for k, tile in enumerate(tiles):
                scaled.append((tile * spread(gains_x[e, :, k * T:(k + 1) * T])).astype(BF16))
            matrix = jnp.concatenate([weights[t * T:(t + 1) * T, :] for t in X_TILES[e]], axis=0)
            extra = dot(jnp.concatenate(scaled, axis=1), matrix)
            add_x(e, near_a, extra[:, 0:T])
            add_x(e, near_h, extra[:, T:])

    def correct_a(v):
        for e in range(2):
            a, h = unpack(recv_y[1, v, e])
            tail = jnp.concatenate([recv_c[1, v, 2 * e], recv_c[1, v, 2 * e + 1]], axis=0)
            add_y(e, far_a, a, tail[:, 0:T])
            add_y(e, far_h, h, tail[:, T:])
        for e in range(2):
            a, h = unpack(recv_x[1, v, e])
            add_x(e, far_a, a)
            add_x(e, far_h, h)

    one = jnp.float32(1.0)
    has_left, has_right = jnp.where(gx > 0, 1.0, 0.0) * one, jnp.where(gx < nx - 1, 1.0, 0.0) * one
    has_down, has_up = jnp.where(gy > 0, 1.0, 0.0) * one, jnp.where(gy < ny - 1, 1.0, 0.0) * one

    def chooser(rows, columns, wanted):
        return jnp.where(iota((rows, columns), 0) == wanted, 1.0, 0.0).astype(BF16)

    lane = iota((U, 2 * T), 1)
    dup = chooser(U, 2 * T, jnp.where(lane < U, lane, lane - HALF))
    dup_back = chooser(U, 2 * T, jnp.where(lane < HALF, lane + T, jnp.where(lane < T, lane + HALF, lane - T)))
    eye = chooser(U, U, iota((U, U), 1))
    solve[...] = dot(sinv[...], dup).astype(BF16)
    solve_n = dot_nt(eye, sinv[...]).astype(BF16)
    solve_t[...] = dot(solve_n, dup_back).astype(BF16)

    adm_high = adm[...].astype(BF16).astype(F32)
    adm_both = jnp.concatenate([adm_high, adm[...] - adm_high], axis=0).astype(BF16)
    adm_table = dot(adm_both, dup).astype(BF16)

    diag = iota((N, N), 0) == iota((N, N), 1)
    spots = [jnp.where(diag, cls[x:x + 1, :].astype(F32), 0.0) for x in range(N)]
    kind = dot(jnp.concatenate(spots, axis=0).astype(BF16), jnp.ones((N, N), BF16))

    def onehot(kinds):
        which = lax.rem(iota((kinds.shape[0], N), 1), 8)
        return jnp.where(which.astype(F32) == kinds, 1.0, 0.0).astype(BF16)

    kind_e = jnp.concatenate(
        [
            jnp.broadcast_to(cls[:, 0:1].astype(F32), (N, N)),
            jnp.broadcast_to(cls[:, N - 1:N].astype(F32), (N, N)),
            kind[0:N],
            kind[ROWS - N:ROWS],
        ],
        axis=0,
    )
    hot, hot_e = onehot(kind), onehot(kind_e)
    admit_e[...] = dot(hot_e, adm_table)
    corner_s[...] = jnp.zeros_like(corner_s)
    no_sender()
    loads[0].wait()
    edge_rows(inc, near_a, near_h, inc_e)
    pick = [
        jnp.where(iota((8, 64), 1) == iota((8, 64), 0) * 8 + slot[:, d:d + 1], 1.0, 0.0)
        for d in range(8)
    ]
    pick = jnp.concatenate(pick, axis=0).astype(BF16)
    gain_dup = dot(gain[...].astype(BF16), dup).astype(BF16)
    table64 = dot(pick, gain_dup)
    pieces = [table64[d * 8:(d + 1) * 8, 0:T] for d in range(8)]
    for d0, d1 in PAIRS:
        pieces.append(jnp.where(low(8), table64[d0 * 8:(d0 + 1) * 8, T:], table64[d1 * 8:(d1 + 1) * 8, T:]))
    table = jnp.concatenate(pieces, axis=1)
    table = jnp.concatenate([table, jnp.zeros_like(table)], axis=0).astype(BF16)
    edge_gain = dot(hot_e, table)
    spot = iota((N, T), 0)

    def along(j):
        return jnp.where((spot + j >= 0) & (spot + j < N), 1.0, 0.0)

    lows = jnp.where(low(N), 1.0, 0.0)
    for e, exists in enumerate((has_down, has_up)):
        raw = edge_gain[e * N:(e + 1) * N]
        first = jnp.where(spot < 8, 1.0, 0.0)
        side = first * has_left + (1.0 - first) * has_right
        for k, t in enumerate(Y_TILES[e]):
            tile = raw[:, t * T:(t + 1) * T]
            ends = jnp.where(spot < 8, jnp.broadcast_to(tile[0:1], (N, T)), jnp.broadcast_to(tile[N - 1:N], (N, T)))
            if k < 3:
                keep = along(k - 1)
                corner = (first, 0.0 * first, 1.0 - first)[k]
            elif k == 3:
                keep = lows * along(-1) + (1.0 - lows) * along(1)
                corner = lows * first + (1.0 - lows) * (1.0 - first)
            else:
                keep = lows if e == 0 else 1.0 - lows
                corner = 0.0 * first
            gains_y[e, 0:N, k * T:(k + 1) * T] = tile * keep * exists
            gains_y[e, N:2 * N, k * T:(k + 1) * T] = ends * corner * side * exists
    for e, exists in enumerate((has_left, has_right)):
        raw = edge_gain[(2 + e) * N:(3 + e) * N]
        for k, t in enumerate(X_TILES[e]):
            keep = along(k % 3 - 1)
            if k >= 3:
                keep = keep * (lows if e == 0 else 1.0 - lows)
            gains_x[e, :, k * T:(k + 1) * T] = raw[:, t * T:(t + 1) * T] * keep * exists

    loads[1].wait()
    weights[...] = jnp.zeros_like(weights)
    for d in range(8):
        weights[d * T:(d + 1) * T, 0:U] = coup[d, 0:T, :]
    for p, (d0, d1) in enumerate(PAIRS):
        base = (8 + p) * T
        weights[base:base + HALF, 0:U] = coup[d0, T:U, :]
        weights[base + HALF:base + T, 0:U] = coup[d1, T:U, :]
    row = iota((2 * T, U), 0)
    place = jnp.where(row < HALF, -1, jnp.where(row < T, row + HALF, row - T))
    order = jnp.where(iota((2 * T, U), 1) == place, 1.0, 0.0).astype(BF16)
    for t in range(TILES):
        weights_t[:, t * T:(t + 1) * T] = dot_nt(order, weights[t * T:(t + 1) * T, 0:U]).astype(BF16)

    loads[2].wait()
    edge_rows(src, far_a, far_h, src_e)

    admit[...] = dot(hot, adm_table)
    stores[2].start()

    def inside(rows, sx, sy):
        r = iota((rows, T), 0)
        x, y = r // N + sx, lax.rem(r, N) + sy
        return (x >= 0) & (x < N) & (y >= 0) & (y < N)

    for t in range(TILES):
        value = dot(hot, table[:, t * T:(t + 1) * T])
        if t < 8:
            keep = jnp.where(inside(ROWS, *STEPS[t]), 1.0, 0.0)
        else:
            d0, d1 = PAIRS[t - 8]
            keep = jnp.where(
                low(ROWS), jnp.where(inside(ROWS, *STEPS[d0]), 1.0, 0.0), jnp.where(inside(ROWS, *STEPS[d1]), 1.0, 0.0)
            )
        gains[:, t * T:(t + 1) * T] = (value * keep).astype(BF16)
        gains_w[:, t * T:(t + 1) * T] = value * keep

    for ref in (v0, vm, vp):
        for r in range(R):
            ref[r, 0:N, :] = jnp.zeros((N, 2 * T), BF16)
            ref[r, (N + 1) * N:(N + 2) * N, :] = jnp.zeros((N, 2 * T), BF16)
    for r in range(R):
        partial[r, 0:N, :] = jnp.zeros((N, TILES * T), F32)
        partial[r, (N + 1) * N:(N + 2) * N, :] = jnp.zeros((N, TILES * T), F32)

    edges_f(0)
    edges_a(0)
    pl.semaphore_wait(barrier, 8)
    start(0, 0)
    start(1, 0)
    main_f()

    def sweep(v, carry):
        main_a()
        arrive(0, v)
        correct_f(v)
        edges_f(v + 1)
        start(0, v + 1)
        main_f()
        arrive(1, v)
        correct_a(v)
        edges_a(v + 1)
        start(1, v + 1)
        return carry

    for v in range(SWEEPS - 1):
        sweep(v, 0)
    main_a()
    arrive(0, SWEEPS - 1)
    correct_f(SWEEPS - 1)
    inc[...] = right_f()
    stores[0].start()
    arrive(1, SWEEPS - 1)
    correct_a(SWEEPS - 1)
    src[...] = right_a()
    stores[1].start()
    for kind in range(2):
        for v in range(SWEEPS):
            sent(kind, v)
    for store in stores:
        store.wait()


def last(rest, back, admit, sinv, cur_out, adj_out):
    cur = dot(rest[...], sinv[...])
    for r in range(R // 2):
        rows = slice(r * ROWS, (r + 1) * ROWS)
        cur_out[rows, :] = (cur[rows] * admit[:, 0:U]).astype(BF16)
    adj_out[...] = dot_nt(back[...], sinv[...]).astype(BF16)


def solution(mesh):
    nx, ny = mesh.shape["gx"], mesh.shape["gy"]

    def local(inc, src, cls, slot, gain, adm, coup, sinv):
        vmem = pl.BlockSpec(memory_space=pltpu.VMEM)
        anywhere = pl.BlockSpec(memory_space=pl.ANY)
        out = jax.ShapeDtypeStruct((R * ROWS, U), BF16)
        rest, back, admit = pl.pallas_call(
            functools.partial(kernel, nx, ny),
            out_shape=(out, out, jax.ShapeDtypeStruct((ROWS, 2 * T), F32)),
            in_specs=[anywhere, anywhere, vmem, vmem, vmem, vmem, anywhere, vmem],
            out_specs=(anywhere, anywhere, anywhere),
            scratch_shapes=[
                pltpu.VMEM((R * ROWS, U), BF16),
                pltpu.VMEM((R * ROWS, U), BF16),
                pltpu.VMEM((8, U, U), BF16),
                pltpu.SemaphoreType.DMA((6,)),
                pltpu.VMEM((ROWS, TILES * T), F32),
                pltpu.VMEM((R, ROWS + 2 * N, 2 * T), BF16),
                pltpu.VMEM((R, ROWS + 2 * N, 2 * T), BF16),
                pltpu.VMEM((R, ROWS + 2 * N, 2 * T), BF16),
                pltpu.VMEM((R * ROWS, 2 * T), BF16),
                pltpu.VMEM((8 * ROWS, T), F32),
                pltpu.VMEM((8 * ROWS, T), F32),
                pltpu.VMEM((8 * ROWS, T), F32),
                pltpu.VMEM((8 * ROWS, T), F32),
                pltpu.VMEM((ROWS, TILES * T), BF16),
                pltpu.VMEM((R * ROWS, TILES * T), BF16),
                pltpu.VMEM((TILES * T, 2 * T), BF16),
                pltpu.VMEM((2 * T, TILES * T), BF16),
                pltpu.VMEM((R, ROWS + 2 * N, TILES * T), F32),
                pltpu.VMEM((ROWS, 2 * T), F32),
                pltpu.VMEM((4 * N, 2 * T), F32),
                pltpu.VMEM((4 * EDGE, 2 * T), F32),
                pltpu.VMEM((4 * EDGE, 2 * T), F32),
                pltpu.VMEM((2, 2 * N, 5 * T), F32),
                pltpu.VMEM((2, N, 6 * T), F32),
                pltpu.VMEM((U, 2 * T), BF16),
                pltpu.VMEM((U, 2 * T), BF16),
                pltpu.VMEM((8, 8 * N, T), F32),
                pltpu.VMEM((2, SWEEPS, 2, EDGE + EDGE // 2, T), BF16),
                pltpu.VMEM((2, SWEEPS, 2, EDGE + EDGE // 2, T), BF16),
                pltpu.VMEM((2, SWEEPS, 4, 8, 2 * T), F32),
                pltpu.VMEM((2, SWEEPS, 2, EDGE + EDGE // 2, T), BF16),
                pltpu.VMEM((2, SWEEPS, 2, EDGE + EDGE // 2, T), BF16),
                pltpu.VMEM((2, SWEEPS, 4, 8, 2 * T), F32),
                pltpu.SemaphoreType.DMA((2, SWEEPS, 8)),
                pltpu.SemaphoreType.DMA((2, SWEEPS, 8)),
            ],
            compiler_params=pltpu.CompilerParams(
                collective_id=0, has_side_effects=True, vmem_limit_bytes=60 * 1024 * 1024
            ),
        )(
            inc.reshape(R * ROWS, U), src.reshape(R * ROWS, U), cls, slot, gain.reshape(64, U), adm, coup, sinv
        )
        half = pl.BlockSpec((R * ROWS // 2, U), lambda i: (i, 0))
        cur, adj = pl.pallas_call(
            last,
            grid=(2,),
            out_shape=(out, out),
            in_specs=[half, half, pl.BlockSpec((ROWS, 2 * T), lambda i: (0, 0)), pl.BlockSpec((U, U), lambda i: (0, 0))],
            out_specs=(half, half),
        )(rest, back, admit, sinv)
        return cur.reshape(R, N, N, U), adj.reshape(R, N, N, U)

    placed = (P(None, "gx", "gy", None), P(None, "gx", "gy", None), P("gx", "gy"), P(), P(), P(), P(), P())
    return jax.shard_map(
        local, mesh=mesh, in_specs=placed, out_specs=(placed[0], placed[0]), check_vma=False
    )
```

```python
import functools

import jax
import jax.numpy as jnp
from jax import lax
from jax.experimental import pallas as pl
from jax.experimental.pallas import tpu as pltpu
from jax.sharding import PartitionSpec as P

MESH = pl.DeviceIdType.MESH
F32 = jnp.float32
BF16 = jnp.bfloat16
SWEEPS = 3
R = 6
N = 16
ROWS = N * N
EDGE = R * N
U = 192
MANY = R * ROWS
T = 128
HALF = 64
STEPS = ((-1, -1), (-1, 0), (-1, 1), (0, -1), (0, 1), (1, -1), (1, 0), (1, 1))
PAIRS = ((0, 5), (1, 6), (2, 7), (3, 4))
TILES = 12
Y_DIRS = ((0, 3, 5), (2, 4, 7))
X_DIRS = ((0, 1, 2), (5, 6, 7))
Y_TILES = ((0, 3, 5, 8, 11), (2, 4, 7, 10, 11))
X_TILES = ((0, 1, 2, 8, 9, 10), (5, 6, 7, 8, 9, 10))


def dot(a, b):
    return jnp.dot(a, b, preferred_element_type=F32)


def dot_nt(a, b):
    return lax.dot_general(a, b, (((1,), (1,)), ((), ())), preferred_element_type=F32)


def iota(shape, dim):
    return lax.broadcasted_iota(jnp.int32, shape, dim)


def low(rows):
    return iota((rows, T), 1) < HALF


def turn(x, shift, axis=0):
    size = x.shape[axis]
    return x if shift % size == 0 else pltpu.roll(x, shift % size, axis)


def spread(tile, corner=None):
    return jnp.concatenate([tile] * R + ([] if corner is None else [corner]), axis=0)


def fold(tile):
    return tile + turn(tile, HALF, 1)


def pack(a, h):
    half = EDGE // 2
    return jnp.concatenate([a, jnp.where(low(half), h[:half], h[half:])], axis=0).astype(BF16)


def unpack(message):
    value = message.astype(F32)
    mixed = value[EDGE:]
    other = turn(mixed, HALF, 1)
    keep = low(EDGE // 2)
    return value[:EDGE], jnp.concatenate([jnp.where(keep, mixed, other), jnp.where(keep, other, mixed)], axis=0)


def kernel(
    nx, ny,
    inc_hbm, src_hbm, cls, slot, gain, adm, coup_hbm, sinv,
    rest_out, back_out, admit_out,
    inc, src, coup, load_sem, gains_w,
    v0, vm, vp, adj, near_a, near_h, far_a, far_h, gains, lhs, weights, weights_t, partial,
    admit, admit_e, inc_e, src_e, gains_y, gains_x, solve, solve_t, corner_s,
    send_y, send_x, send_c, recv_y, recv_x, recv_c,
    send_sem, recv_sem,
):
    gx, gy = lax.axis_index("gx"), lax.axis_index("gy")
    left, right = lax.rem(gx + nx - 1, nx), lax.rem(gx + 1, nx)
    down, up = lax.rem(gy + ny - 1, ny), lax.rem(gy + 1, ny)
    y_to = ((gx, down), (gx, up))
    x_to = ((left, gy), (right, gy))
    c_to = ((left, down), (right, down), (left, up), (right, up))

    barrier = pltpu.get_barrier_semaphore()
    for where in y_to + x_to + c_to:
        pl.semaphore_signal(barrier, inc=1, device_id=where, device_id_type=MESH)

    loads = [
        pltpu.make_async_copy(a, b, load_sem.at[k])
        for k, (a, b) in enumerate(((inc_hbm, inc), (coup_hbm, coup), (src_hbm, src)))
    ]
    stores = [
        pltpu.make_async_copy(a, b, load_sem.at[3 + k])
        for k, (a, b) in enumerate(((inc, rest_out), (src, back_out), (admit, admit_out)))
    ]
    for load in loads:
        load.start()

    def take(ref):
        parts = [ref[pl.ds(e * (N - 1), EDGE, stride=N), :] for e in range(2)]
        for e in range(2):
            for r in range(R):
                start = r * ROWS + e * (ROWS - N)
                parts.append(ref[start:start + N, :])
        return jnp.concatenate(parts, axis=0)

    def edge_rows(data, a_ref, h_ref, e_ref):
        h_ref[...] = jnp.zeros_like(h_ref)
        for r in range(R):
            a_ref[r * ROWS:(r + 1) * ROWS, :] = data[r * ROWS:(r + 1) * ROWS, 0:T].astype(F32)
            h_ref[r * ROWS:(r + 1) * ROWS, 0:HALF] = data[r * ROWS:(r + 1) * ROWS, T:U].astype(F32)
        for k, ref in enumerate((a_ref, h_ref)):
            columns = slice(k * T, (k + 1) * T)
            e_ref[:, columns] = take(ref)
            ref[...] = jnp.zeros_like(ref)

    def scale_e():
        return jnp.concatenate([spread(admit_e[e * N:(e + 1) * N, :]) for e in range(4)], axis=0)

    def corners(k, value):
        corner_s[k, 0:EDGE, :] = value
        return jnp.concatenate([corner_s[k, pl.ds(0, 8, stride=N), :], corner_s[k, pl.ds(N - 1, 8, stride=N), :]], axis=0)

    def edges_f(v):
        near_e = jnp.concatenate([take(near_a), take(near_h)], axis=1)
        rest = (inc_e[...] - near_e).astype(BF16)
        cur_e = dot(rest[:, 0:U], solve[...]) * scale_e()
        for e in range(2):
            rows = slice(e * EDGE, (e + 1) * EDGE)
            send_y[0, v, e] = pack(cur_e[rows, 0:T], cur_e[rows, T:])
            both = jnp.concatenate([corners(2 * e, cur_e[rows, 0:T]), corners(2 * e + 1, cur_e[rows, T:])], axis=1)
            send_c[0, v, 2 * e] = both[0:8]
            send_c[0, v, 2 * e + 1] = both[8:16]
        for e in range(2):
            rows = slice((2 + e) * EDGE, (3 + e) * EDGE)
            send_x[0, v, e] = pack(cur_e[rows, 0:T], cur_e[rows, T:])

    def products(state, tiles):
        out = []
        for k in range(0, len(tiles), 2):
            two = tiles[k:k + 2]
            value = dot(state, jnp.concatenate([weights_t[:, t * T:(t + 1) * T] for t in two], axis=1))
            out += [value[:, i * T:(i + 1) * T] for i in range(len(two))]
        return out

    def edges_a(v):
        far_e = jnp.concatenate([take(far_a), take(far_h)], axis=1)
        back = ((src_e[...] - far_e) * scale_e()).astype(BF16)
        adj_e = dot(back[:, 0:U], solve_t[...])
        for e in range(2):
            rows = slice(e * EDGE, (e + 1) * EDGE)
            cut = [corners(4 + 2 * e + k, adj_e[rows, k * T:(k + 1) * T]) for k in range(2)]
            state = jnp.concatenate([adj_e[rows], jnp.concatenate(cut, axis=1)], axis=0).astype(BF16)
            out = []
            for k, value in enumerate(products(state, Y_TILES[e])):
                gain_k = gains_y[e, :, k * T:(k + 1) * T]
                out.append(value * spread(gain_k[0:N], gain_k[N:]))
            part_a = turn(out[0][:EDGE], -1) + out[1][:EDGE] + turn(out[2][:EDGE], 1)
            part_h = fold(
                jnp.where(low(EDGE), turn(out[3][:EDGE], -1), turn(out[3][:EDGE], 1)) + out[4][:EDGE]
            )
            tail_a = out[0][EDGE:] + out[1][EDGE:] + out[2][EDGE:]
            tail_h = fold(out[3][EDGE:] + out[4][EDGE:])
            send_y[1, v, e] = pack(part_a, part_h)
            tail = jnp.concatenate([tail_a, tail_h], axis=1)
            send_c[1, v, 2 * e] = tail[0:8]
            send_c[1, v, 2 * e + 1] = tail[8:16]
        for e in range(2):
            state = adj_e[(2 + e) * EDGE:(3 + e) * EDGE].astype(BF16)
            out = []
            for k, value in enumerate(products(state, X_TILES[e])):
                out.append(value * spread(gains_x[e, :, k * T:(k + 1) * T]))
            part_a = turn(out[0], -1) + out[1] + turn(out[2], 1)
            part_h = fold(turn(out[3], -1) + out[4] + turn(out[5], 1))
            send_x[1, v, e] = pack(part_a, part_h)

    inside_y = (gy > 0, gy < ny - 1)
    inside_x = (gx > 0, gx < nx - 1)

    def copies(kind, v):
        made = []
        for e in range(2):
            made.append((send_y.at[kind, v, e], recv_y.at[kind, v, 1 - e], y_to[e], e, 1 - e, inside_y[e], inside_y[1 - e]))
        for e in range(2):
            made.append((send_x.at[kind, v, e], recv_x.at[kind, v, 1 - e], x_to[e], 2 + e, 3 - e, inside_x[e], inside_x[1 - e]))
        for q in range(4):
            goes = inside_y[q // 2] & inside_x[q % 2]
            comes = inside_y[1 - q // 2] & inside_x[1 - q % 2]
            made.append((send_c.at[kind, v, q], recv_c.at[kind, v, 3 - q], c_to[q], 4 + q, 7 - q, goes, comes))
        return [
            (
                pltpu.make_async_remote_copy(
                    src_ref=a, dst_ref=b, send_sem=send_sem.at[kind, v, s], recv_sem=recv_sem.at[kind, v, t],
                    device_id=where, device_id_type=MESH,
                ),
                goes,
                comes,
            )
            for a, b, where, s, t, goes, comes in made
        ]

    def start(kind, v):
        for copy, goes, _ in copies(kind, v):
            pl.when(goes)(copy.start)

    def arrive(kind, v):
        for copy, _, comes in copies(kind, v):
            pl.when(comes)(copy.wait_recv)

    def sent(kind, v):
        for copy, goes, _ in copies(kind, v):
            pl.when(goes)(copy.wait_send)

    def no_sender():
        def clear(ref, q):
            for kind in range(2):
                for v in range(SWEEPS):
                    ref[kind, v, q] = jnp.zeros(ref.shape[3:], ref.dtype)

        for e in range(2):
            pl.when(jnp.logical_not(inside_y[e]))(functools.partial(clear, recv_y, e))
            pl.when(jnp.logical_not(inside_x[e]))(functools.partial(clear, recv_x, e))
        for q in range(4):
            pl.when(jnp.logical_not(inside_y[q // 2] & inside_x[q % 2]))(functools.partial(clear, recv_c, q))

    def right_f():
        near = jnp.concatenate([near_a[0:MANY, :], near_h[0:MANY, 0:HALF]], axis=1)
        return (inc[...].astype(F32) - near).astype(BF16)

    def right_a():
        far = jnp.concatenate([far_a[0:MANY, :], far_h[0:MANY, 0:HALF]], axis=1)
        back = src[...].astype(F32) - far
        back = [back[r * ROWS:(r + 1) * ROWS] * admit[:, 0:U] for r in range(R)]
        return jnp.concatenate(back, axis=0).astype(BF16)

    shifted = {-1: vm, 0: v0, 1: vp}

    halves = (slice(0, MANY // 2), slice(MANY // 2, MANY))

    def main_f():
        rest = right_f()
        cur = jnp.concatenate([dot(rest[rows], solve[...]) for rows in halves], axis=0)
        for r in range(R):
            one_cur = cur[r * ROWS:(r + 1) * ROWS] * admit[...]
            v0[r, N:N + ROWS, :] = one_cur.astype(BF16)
            vm[r, N:N + ROWS, :] = turn(one_cur, 1).astype(BF16)
            vp[r, N:N + ROWS, :] = turn(one_cur, -1).astype(BF16)
        for r in range(R):
            rows = slice(r * ROWS, (r + 1) * ROWS)

            def nearby(d, columns):
                sx, sy = STEPS[d]
                return shifted[sy][r, N * (1 + sx):N * (1 + sx) + ROWS, columns]

            for d in range(8):
                columns = slice(d * T, (d + 1) * T)
                lhs[rows, columns] = nearby(d, slice(0, T)) * gains[:, columns]
            for p, (d0, d1) in enumerate(PAIRS):
                columns = slice((8 + p) * T, (9 + p) * T)
                both = jnp.where(low(ROWS), nearby(d0, slice(T, 2 * T)), nearby(d1, slice(T, 2 * T)))
                lhs[rows, columns] = both * gains[:, columns]
        for rows in halves:
            near = dot(lhs[rows, :], weights[...])
            near_a[rows, :] = near[:, 0:T]
            near_h[rows, :] = near[:, T:]

    def main_a():
        back = right_a()
        for rows in halves:
            adj[rows, :] = dot(back[rows], solve_t[...]).astype(BF16)
        for t in range(TILES // 2):
            columns = slice(2 * t * T, 2 * (t + 1) * T)
            value = dot(adj[...], weights_t[:, columns])
            for r in range(R):
                partial[r, N:N + ROWS, columns] = value[r * ROWS:(r + 1) * ROWS] * gains_w[:, columns]
        for r in range(R):

            def part(x, t):
                return partial[r, x * N:(x + 1) * N, t * T:(t + 1) * T]

            for x in range(N):
                sums = {sy: None for sy in (-1, 0, 1)}
                for d, (sx, sy) in enumerate(STEPS):
                    value = part(1 + x - sx, d)
                    sums[sy] = value if sums[sy] is None else sums[sy] + value
                a = turn(sums[1], 1) + sums[0] + turn(sums[-1], -1)
                tops = {sy: jnp.where(low(N), part(2 + x, 9 + sy), part(x, 9 + sy)) for sy in (-1, 0, 1)}
                mid = part(1 + x, 11)
                below = tops[-1] + jnp.where(low(N), mid, 0.0)
                above = tops[1] + jnp.where(low(N), 0.0, mid)
                h = fold(turn(above, 1) + tops[0] + turn(below, -1))
                at = r * ROWS + x * N
                far_a[at:at + N, :] = a
                far_h[at:at + N, :] = h

    def add_y(e, ref, value, tail):
        y0 = e * (N - 1)
        for at, piece in (
            (pl.ds(y0, EDGE, stride=N), value),
            (pl.ds(y0, 8, stride=ROWS), tail[0:8]),
            (pl.ds(y0 + ROWS - N, 8, stride=ROWS), tail[8:16]),
        ):
            ref[at, :] = ref[at, :] + piece

    def add_x(e, ref, value):
        for r in range(R):
            at = r * ROWS + e * (ROWS - N)
            ref[at:at + N, :] = ref[at:at + N, :] + value[r * N:(r + 1) * N]

    def correct_f(v):
        for e in range(2):
            a, h = unpack(recv_y[0, v, e])
            tail = jnp.concatenate([recv_c[0, v, 2 * e], recv_c[0, v, 2 * e + 1]], axis=0)
            tail_a, tail_h = tail[:, 0:T], tail[:, T:]
            tiles = [
                (turn(a, 1), tail_a), (a, tail_a), (turn(a, -1), tail_a),
                (jnp.where(low(EDGE), turn(h, 1), turn(h, -1)), tail_h), (h, tail_h),
            ]
            scaled = []
            for k, tile in enumerate(tiles):
                gain_k = gains_y[e, :, k * T:(k + 1) * T]
                scaled.append((jnp.concatenate(tile, axis=0) * spread(gain_k[0:N], gain_k[N:])).astype(BF16))
            matrix = jnp.concatenate([weights[t * T:(t + 1) * T, :] for t in Y_TILES[e]], axis=0)
            extra = dot(jnp.concatenate(scaled, axis=1), matrix)
            add_y(e, near_a, extra[:EDGE, 0:T], extra[EDGE:, 0:T])
            add_y(e, near_h, extra[:EDGE, T:], extra[EDGE:, T:])
        for e in range(2):
            a, h = unpack(recv_x[0, v, e])
            tiles = [turn(a, 1), a, turn(a, -1), turn(h, 1), h, turn(h, -1)]
            scaled = []
            for k, tile in enumerate(tiles):
                scaled.append((tile * spread(gains_x[e, :, k * T:(k + 1) * T])).astype(BF16))
            matrix = jnp.concatenate([weights[t * T:(t + 1) * T, :] for t in X_TILES[e]], axis=0)
            extra = dot(jnp.concatenate(scaled, axis=1), matrix)
            add_x(e, near_a, extra[:, 0:T])
            add_x(e, near_h, extra[:, T:])

    def correct_a(v):
        for e in range(2):
            a, h = unpack(recv_y[1, v, e])
            tail = jnp.concatenate([recv_c[1, v, 2 * e], recv_c[1, v, 2 * e + 1]], axis=0)
            add_y(e, far_a, a, tail[:, 0:T])
            add_y(e, far_h, h, tail[:, T:])
        for e in range(2):
            a, h = unpack(recv_x[1, v, e])
            add_x(e, far_a, a)
            add_x(e, far_h, h)

    one = jnp.float32(1.0)
    has_left, has_right = jnp.where(gx > 0, 1.0, 0.0) * one, jnp.where(gx < nx - 1, 1.0, 0.0) * one
    has_down, has_up = jnp.where(gy > 0, 1.0, 0.0) * one, jnp.where(gy < ny - 1, 1.0, 0.0) * one

    def chooser(rows, columns, wanted):
        return jnp.where(iota((rows, columns), 0) == wanted, 1.0, 0.0).astype(BF16)

    lane = iota((U, 2 * T), 1)
    dup = chooser(U, 2 * T, jnp.where(lane < U, lane, lane - HALF))
    dup_back = chooser(U, 2 * T, jnp.where(lane < HALF, lane + T, jnp.where(lane < T, lane + HALF, lane - T)))
    eye = chooser(U, U, iota((U, U), 1))
    solve[...] = dot(sinv[...], dup).astype(BF16)
    solve_n = dot_nt(eye, sinv[...]).astype(BF16)
    solve_t[...] = dot(solve_n, dup_back).astype(BF16)

    adm_high = adm[...].astype(BF16).astype(F32)
    adm_both = jnp.concatenate([adm_high, adm[...] - adm_high], axis=0).astype(BF16)
    adm_table = dot(adm_both, dup).astype(BF16)

    diag = iota((N, N), 0) == iota((N, N), 1)
    spots = [jnp.where(diag, cls[x:x + 1, :].astype(F32), 0.0) for x in range(N)]
    kind = dot(jnp.concatenate(spots, axis=0).astype(BF16), jnp.ones((N, N), BF16))

    def onehot(kinds):
        which = lax.rem(iota((kinds.shape[0], N), 1), 8)
        return jnp.where(which.astype(F32) == kinds, 1.0, 0.0).astype(BF16)

    kind_e = jnp.concatenate(
        [
            jnp.broadcast_to(cls[:, 0:1].astype(F32), (N, N)),
            jnp.broadcast_to(cls[:, N - 1:N].astype(F32), (N, N)),
            kind[0:N],
            kind[ROWS - N:ROWS],
        ],
        axis=0,
    )
    hot, hot_e = onehot(kind), onehot(kind_e)
    admit_e[...] = dot(hot_e, adm_table)
    corner_s[...] = jnp.zeros_like(corner_s)
    no_sender()
    loads[0].wait()
    edge_rows(inc, near_a, near_h, inc_e)
    pick = [
        jnp.where(iota((8, 64), 1) == iota((8, 64), 0) * 8 + slot[:, d:d + 1], 1.0, 0.0)
        for d in range(8)
    ]
    pick = jnp.concatenate(pick, axis=0).astype(BF16)
    gain_dup = dot(gain[...].astype(BF16), dup).astype(BF16)
    table64 = dot(pick, gain_dup)
    pieces = [table64[d * 8:(d + 1) * 8, 0:T] for d in range(8)]
    for d0, d1 in PAIRS:
        pieces.append(jnp.where(low(8), table64[d0 * 8:(d0 + 1) * 8, T:], table64[d1 * 8:(d1 + 1) * 8, T:]))
    table = jnp.concatenate(pieces, axis=1)
    table = jnp.concatenate([table, jnp.zeros_like(table)], axis=0).astype(BF16)
    edge_gain = dot(hot_e, table)
    spot = iota((N, T), 0)

    def along(j):
        return jnp.where((spot + j >= 0) & (spot + j < N), 1.0, 0.0)

    lows = jnp.where(low(N), 1.0, 0.0)
    for e, exists in enumerate((has_down, has_up)):
        raw = edge_gain[e * N:(e + 1) * N]
        first = jnp.where(spot < 8, 1.0, 0.0)
        side = first * has_left + (1.0 - first) * has_right
        for k, t in enumerate(Y_TILES[e]):
            tile = raw[:, t * T:(t + 1) * T]
            ends = jnp.where(spot < 8, jnp.broadcast_to(tile[0:1], (N, T)), jnp.broadcast_to(tile[N - 1:N], (N, T)))
            if k < 3:
                keep = along(k - 1)
                corner = (first, 0.0 * first, 1.0 - first)[k]
            elif k == 3:
                keep = lows * along(-1) + (1.0 - lows) * along(1)
                corner = lows * first + (1.0 - lows) * (1.0 - first)
            else:
                keep = lows if e == 0 else 1.0 - lows
                corner = 0.0 * first
            gains_y[e, 0:N, k * T:(k + 1) * T] = tile * keep * exists
            gains_y[e, N:2 * N, k * T:(k + 1) * T] = ends * corner * side * exists
    for e, exists in enumerate((has_left, has_right)):
        raw = edge_gain[(2 + e) * N:(3 + e) * N]
        for k, t in enumerate(X_TILES[e]):
            keep = along(k % 3 - 1)
            if k >= 3:
                keep = keep * (lows if e == 0 else 1.0 - lows)
            gains_x[e, :, k * T:(k + 1) * T] = raw[:, t * T:(t + 1) * T] * keep * exists

    loads[1].wait()
    weights[...] = jnp.zeros_like(weights)
    for d in range(8):
        weights[d * T:(d + 1) * T, 0:U] = coup[d, 0:T, :]
    for p, (d0, d1) in enumerate(PAIRS):
        base = (8 + p) * T
        weights[base:base + HALF, 0:U] = coup[d0, T:U, :]
        weights[base + HALF:base + T, 0:U] = coup[d1, T:U, :]
    row = iota((2 * T, U), 0)
    place = jnp.where(row < HALF, -1, jnp.where(row < T, row + HALF, row - T))
    order = jnp.where(iota((2 * T, U), 1) == place, 1.0, 0.0).astype(BF16)
    for t in range(TILES):
        weights_t[:, t * T:(t + 1) * T] = dot_nt(order, weights[t * T:(t + 1) * T, 0:U]).astype(BF16)

    loads[2].wait()
    edge_rows(src, far_a, far_h, src_e)

    admit[...] = dot(hot, adm_table)
    stores[2].start()

    def inside(rows, sx, sy):
        r = iota((rows, T), 0)
        x, y = r // N + sx, lax.rem(r, N) + sy
        return (x >= 0) & (x < N) & (y >= 0) & (y < N)

    for t in range(TILES):
        value = dot(hot, table[:, t * T:(t + 1) * T])
        if t < 8:
            keep = jnp.where(inside(ROWS, *STEPS[t]), 1.0, 0.0)
        else:
            d0, d1 = PAIRS[t - 8]
            keep = jnp.where(
                low(ROWS), jnp.where(inside(ROWS, *STEPS[d0]), 1.0, 0.0), jnp.where(inside(ROWS, *STEPS[d1]), 1.0, 0.0)
            )
        gains[:, t * T:(t + 1) * T] = (value * keep).astype(BF16)
        gains_w[:, t * T:(t + 1) * T] = value * keep

    for ref in (v0, vm, vp):
        for r in range(R):
            ref[r, 0:N, :] = jnp.zeros((N, 2 * T), BF16)
            ref[r, (N + 1) * N:(N + 2) * N, :] = jnp.zeros((N, 2 * T), BF16)
    for r in range(R):
        partial[r, 0:N, :] = jnp.zeros((N, TILES * T), F32)
        partial[r, (N + 1) * N:(N + 2) * N, :] = jnp.zeros((N, TILES * T), F32)

    edges_f(0)
    edges_a(0)
    pl.semaphore_wait(barrier, 8)
    start(0, 0)
    main_f()
    start(1, 0)

    def sweep(v, carry):
        main_a()
        arrive(0, v)
        correct_f(v)
        edges_f(v + 1)
        start(0, v + 1)
        main_f()
        arrive(1, v)
        correct_a(v)
        edges_a(v + 1)
        start(1, v + 1)
        return carry

    for v in range(SWEEPS - 1):
        sweep(v, 0)
    main_a()
    arrive(0, SWEEPS - 1)
    correct_f(SWEEPS - 1)
    step = 2 * N
    for k in range(MANY // step):
        at = slice(k * step, (k + 1) * step)
        near = jnp.concatenate([near_a[at, :], near_h[at, 0:HALF]], axis=1)
        inc[at, :] = (inc[at, :].astype(F32) - near).astype(BF16)
    stores[0].start()
    arrive(1, SWEEPS - 1)
    correct_a(SWEEPS - 1)
    for k in range(MANY // step):
        at = slice(k * step, (k + 1) * step)
        scale = admit[(k * step) % ROWS:(k * step) % ROWS + step, 0:U]
        far = jnp.concatenate([far_a[at, :], far_h[at, 0:HALF]], axis=1)
        src[at, :] = ((src[at, :].astype(F32) - far) * scale).astype(BF16)
    stores[1].start()
    for kind in range(2):
        for v in range(SWEEPS):
            sent(kind, v)
    for store in stores:
        store.wait()


def last(rest, back, admit, sinv, cur_out, adj_out):
    cur = dot(rest[...], sinv[...])
    for r in range(R // 2):
        rows = slice(r * ROWS, (r + 1) * ROWS)
        cur_out[rows, :] = (cur[rows] * admit[:, 0:U]).astype(BF16)
    adj_out[...] = dot_nt(back[...], sinv[...]).astype(BF16)


def solution(mesh):
    nx, ny = mesh.shape["gx"], mesh.shape["gy"]

    def local(inc, src, cls, slot, gain, adm, coup, sinv):
        vmem = pl.BlockSpec(memory_space=pltpu.VMEM)
        anywhere = pl.BlockSpec(memory_space=pl.ANY)
        out = jax.ShapeDtypeStruct((R * ROWS, U), BF16)
        rest, back, admit = pl.pallas_call(
            functools.partial(kernel, nx, ny),
            out_shape=(out, out, jax.ShapeDtypeStruct((ROWS, 2 * T), F32)),
            in_specs=[anywhere, anywhere, vmem, vmem, vmem, vmem, anywhere, vmem],
            out_specs=(anywhere, anywhere, anywhere),
            scratch_shapes=[
                pltpu.VMEM((R * ROWS, U), BF16),
                pltpu.VMEM((R * ROWS, U), BF16),
                pltpu.VMEM((8, U, U), BF16),
                pltpu.SemaphoreType.DMA((6,)),
                pltpu.VMEM((ROWS, TILES * T), F32),
                pltpu.VMEM((R, ROWS + 2 * N, 2 * T), BF16),
                pltpu.VMEM((R, ROWS + 2 * N, 2 * T), BF16),
                pltpu.VMEM((R, ROWS + 2 * N, 2 * T), BF16),
                pltpu.VMEM((R * ROWS, 2 * T), BF16),
                pltpu.VMEM((8 * ROWS, T), F32),
                pltpu.VMEM((8 * ROWS, T), F32),
                pltpu.VMEM((8 * ROWS, T), F32),
                pltpu.VMEM((8 * ROWS, T), F32),
                pltpu.VMEM((ROWS, TILES * T), BF16),
                pltpu.VMEM((R * ROWS, TILES * T), BF16),
                pltpu.VMEM((TILES * T, 2 * T), BF16),
                pltpu.VMEM((2 * T, TILES * T), BF16),
                pltpu.VMEM((R, ROWS + 2 * N, TILES * T), F32),
                pltpu.VMEM((ROWS, 2 * T), F32),
                pltpu.VMEM((4 * N, 2 * T), F32),
                pltpu.VMEM((4 * EDGE, 2 * T), F32),
                pltpu.VMEM((4 * EDGE, 2 * T), F32),
                pltpu.VMEM((2, 2 * N, 5 * T), F32),
                pltpu.VMEM((2, N, 6 * T), F32),
                pltpu.VMEM((U, 2 * T), BF16),
                pltpu.VMEM((U, 2 * T), BF16),
                pltpu.VMEM((8, 8 * N, T), F32),
                pltpu.VMEM((2, SWEEPS, 2, EDGE + EDGE // 2, T), BF16),
                pltpu.VMEM((2, SWEEPS, 2, EDGE + EDGE // 2, T), BF16),
                pltpu.VMEM((2, SWEEPS, 4, 8, 2 * T), F32),
                pltpu.VMEM((2, SWEEPS, 2, EDGE + EDGE // 2, T), BF16),
                pltpu.VMEM((2, SWEEPS, 2, EDGE + EDGE // 2, T), BF16),
                pltpu.VMEM((2, SWEEPS, 4, 8, 2 * T), F32),
                pltpu.SemaphoreType.DMA((2, SWEEPS, 8)),
                pltpu.SemaphoreType.DMA((2, SWEEPS, 8)),
            ],
            compiler_params=pltpu.CompilerParams(
                collective_id=0, has_side_effects=True, vmem_limit_bytes=60 * 1024 * 1024
            ),
        )(
            inc.reshape(R * ROWS, U), src.reshape(R * ROWS, U), cls, slot, gain.reshape(64, U), adm, coup, sinv
        )
        half = pl.BlockSpec((R * ROWS // 2, U), lambda i: (i, 0))
        cur, adj = pl.pallas_call(
            last,
            grid=(2,),
            out_shape=(out, out),
            in_specs=[half, half, pl.BlockSpec((ROWS, 2 * T), lambda i: (0, 0)), pl.BlockSpec((U, U), lambda i: (0, 0))],
            out_specs=(half, half),
        )(rest, back, admit, sinv)
        return cur.reshape(R, N, N, U), adj.reshape(R, N, N, U)

    placed = (P(None, "gx", "gy", None), P(None, "gx", "gy", None), P("gx", "gy"), P(), P(), P(), P(), P())
    return jax.shard_map(
        local, mesh=mesh, in_specs=placed, out_specs=(placed[0], placed[0]), check_vma=False
    )
```
